256 devices in a mesh: seq: 64 (over z, y, core), head: 4 (over x).
Axes of the slice: x: 4, y: 4, z: 8, core: 2. Of those that a mesh axis runs over, the one named last changes fastest.
Arguments:
- queries: bfloat16 [65536, 1024], P('seq', 'head'), may hold values from -0.69921875 to 0.69921875
- key_vectors: bfloat16 [65536, 1024], P('seq', 'head'), may hold values from -0.69921875 to 0.69921875
- values: bfloat16 [65536, 1024], P('seq', 'head'), may hold values from -0.69921875 to 0.69921875
- out_grad: bfloat16 [65536, 1024], P('seq', 'head'), may hold values from -6 to 6
- level_coef: float32 [17, 65536], P(None, 'seq'), may hold values from 0.25 to 4
- saved_states: bfloat16 [64, 6, 8, 128, 128], P('seq', None, 'head'), may hold values from -0.079589844 to 0.079589844
Outputs:
- query_grad: bfloat16 [65536, 1024], P('seq', 'head')
- key_grad: bfloat16 [65536, 1024], P('seq', 'head')
- value_grad: bfloat16 [65536, 1024], P('seq', 'head')
- coef_grad: float32 [17, 65536], P(None, 'seq')
The draws below stay inside these ranges and needn't reach their ends.
All inputs are finite; a program needn't handle non-finite values.
Results may differ from the reference program's by a relative error of at most 0.0053.
Values sent between devices are 32-bit elements; how exact they have to be, the bound alone decides.
A program may use at most 128 MiB of HBM per device.

```python
import math
import jax
import jax.numpy as jnp
import numpy as np
from jax import lax

HEADS = 8
DK = 128
DV = 128
LOCAL_LEVELS = 11
CROSS_LEVELS = 6
SHARD_TOKENS = 1024
SHARDS = 64
TOKENS = 65536
LEVELS = 17


def steps_of(stream_key, shape, shards, least, high):
    def one(axis_at, shards_of):
        draws = jax.random.uniform(jax.random.fold_in(jax.random.fold_in(stream_key, 6), axis_at), (shards_of,), jnp.float32, least / len(shards), high / len(shards))
        return jnp.repeat(jnp.exp(draws), shape[axis_at] // shards_of).reshape((-1,) + (1,) * (len(shape) - axis_at - 1))

    gain = one(*shards[0])
    for cut in shards[1:]:
        gain = gain * one(*cut)
    return gain


def centred(own_key, shape, width, bound, split=(), kind=jnp.bfloat16):
    result = width * jax.random.normal(own_key, shape, jnp.float32)
    if split:
        result = result * steps_of(own_key, shape, split, -0.22, 0.18)
    return jnp.clip(result, -bound, bound).astype(kind)


def setup_inputs(seed: int = 0) -> dict:
    splits = jax.random.split(jax.random.key(seed), 7)
    queries = centred(splits[0], (TOKENS, HEADS * DK), 0.115, 0.69921875, ((0, 64), (1, 4)))
    key_vectors = centred(splits[1], (TOKENS, HEADS * DK), 0.115, 0.69921875, ((0, 64), (1, 4)))
    values = centred(splits[2], (TOKENS, HEADS * DV), 0.115, 0.69921875, ((0, 64), (1, 4)))
    out_grad = centred(splits[3], (TOKENS, HEADS * DV), 1.0, 6.0, ((0, 64), (1, 4)))
    level_coef = jnp.clip(jnp.exp(math.log(4.0) - 2.7725887 * jax.random.uniform(splits[4], (LEVELS, TOKENS), jnp.float32) ** steps_of(splits[4], (LEVELS, TOKENS), ((1, 64),), -0.2, 0.2)), 0.25, 4.0)
    saved_states = centred(splits[5], (SHARDS, CROSS_LEVELS, HEADS, DK, DV), 0.013, 0.079589844, ((0, 64), (2, 4)))
    return {"queries": queries, "key_vectors": key_vectors, "values": values, "out_grad": out_grad, "level_coef": level_coef, "saved_states": saved_states}


def level_weight(level_idx):
    if level_idx == 0:
        return 1.0
    return 2.0 ** (-(level_idx - 1) / 2.0)


def level_table(row_pos, col_pos, local_levels):
    mixed = jnp.bitwise_xor(row_pos[:, None], col_pos[None, :])
    levels = jnp.zeros(mixed.shape, jnp.int32)
    for bit_pos in range(local_levels - 1):
        levels = levels + (jnp.right_shift(mixed, bit_pos) > 0).astype(jnp.int32)
    return levels


def coef_table(levels, gate_rows, local_levels):
    level_mix = jnp.zeros(levels.shape, jnp.float32)
    for level_idx in range(local_levels):
        level_mix = jnp.where(levels == level_idx, gate_rows[level_idx][:, None] * level_weight(level_idx), level_mix)
    return level_mix


def rounded(array_in):
    return lax.optimization_barrier(array_in.astype(jnp.bfloat16)).astype(jnp.float32)


def one_shard(packed):
    query_heads, key_heads, value_heads, grad_heads, gates_here, states, shard_idx = packed
    query_data = query_heads.astype(jnp.float32)
    key_data = key_heads.astype(jnp.float32)
    value_data = value_heads.astype(jnp.float32)
    grad_data = grad_heads.astype(jnp.float32)
    positions = jnp.arange(SHARD_TOKENS, dtype=jnp.int32)
    levels = level_table(positions, positions, LOCAL_LEVELS)
    causal = positions[None, :] <= positions[:, None]
    level_mix = jnp.where(causal, coef_table(levels, gates_here[:LOCAL_LEVELS], LOCAL_LEVELS), 0.0)
    scores = jnp.einsum("thd,shd->hts", query_data, key_data)
    grad_scores = jnp.einsum("the,she->hts", grad_data, value_data)
    grad_weights = rounded(level_mix[None] * grad_scores)
    weights = rounded(level_mix[None] * scores)
    query_local = jnp.einsum("hts,shd->thd", grad_weights, key_data)
    key_local = jnp.einsum("hts,thd->shd", grad_weights, query_data)
    value_local = jnp.einsum("hts,the->she", weights, grad_data)
    products = jnp.where(causal, jnp.sum(scores * grad_scores, axis=0), 0.0)
    local_grads = jnp.stack([level_weight(level_idx) * jnp.sum(jnp.where(levels == level_idx, products, 0.0), axis=1) for level_idx in range(LOCAL_LEVELS)])
    level_ids = jnp.arange(CROSS_LEVELS, dtype=jnp.int32)
    bit_flags = jnp.bitwise_and(jnp.right_shift(shard_idx, level_ids), 1).astype(jnp.float32)
    cross_gates = gates_here[LOCAL_LEVELS:]
    scaled = rounded(cross_gates[:, :, None, None] * grad_data[None])
    state_grads = jnp.einsum("thd,jthe->jhde", query_data, scaled)
    weight_list = jnp.array([level_weight(LOCAL_LEVELS + level_idx) for level_idx in range(CROSS_LEVELS)], jnp.float32)
    contrib = state_grads * (weight_list * bit_flags)[:, None, None, None]
    projected = jnp.einsum("the,jhde->jthd", grad_data, states.astype(jnp.float32))
    gate_rows = cross_gates * bit_flags[:, None]
    query_grad = query_local + jnp.sum(gate_rows[:, :, None, None] * projected, axis=0)
    cross_grads = bit_flags[:, None] * jnp.sum(projected * query_data[None], axis=(2, 3))
    coef_grad = jnp.concatenate([local_grads, cross_grads], axis=0)
    return query_grad, key_local, value_local, coef_grad, contrib


def reference(queries, key_vectors, values, out_grad, level_coef, saved_states):
    query_heads = queries.reshape(SHARDS, SHARD_TOKENS, HEADS, DK)
    key_heads = key_vectors.reshape(SHARDS, SHARD_TOKENS, HEADS, DK)
    value_heads = values.reshape(SHARDS, SHARD_TOKENS, HEADS, DV)
    grad_heads = out_grad.reshape(SHARDS, SHARD_TOKENS, HEADS, DV)
    gates = level_coef.reshape(LEVELS, SHARDS, SHARD_TOKENS).transpose(1, 0, 2)
    results = lax.map(one_shard, (query_heads, key_heads, value_heads, grad_heads, gates, saved_states, jnp.arange(SHARDS, dtype=jnp.int32)))
    query_grad, key_local, value_local, coef_parts, contrib = results
    grad_state = jnp.zeros((SHARDS, HEADS, DK, DV), jnp.float32)
    shard_ids = np.arange(SHARDS)
    for level_idx in range(CROSS_LEVELS):
        group_size = 2 ** level_idx
        if 2 * group_size <= SHARDS:
            block_sums = contrib[:, level_idx].reshape(SHARDS // group_size, group_size, HEADS, DK, DV).sum(axis=1)
            partner = ((shard_ids >> level_idx) | 1).astype(np.int32)
            receives = ((shard_ids >> level_idx) & 1) == 0
            grad_state = grad_state + jnp.where(jnp.asarray(receives)[:, None, None, None], block_sums[jnp.asarray(partner)], 0.0)
    state_data = rounded(grad_state)
    key_grad = key_local + jnp.einsum("bshe,bhde->bshd", value_heads.astype(jnp.float32), state_data)
    value_grad = value_local + jnp.einsum("bshd,bhde->bshe", key_heads.astype(jnp.float32), state_data)
    return (query_grad.astype(jnp.bfloat16).reshape(TOKENS, HEADS * DK),
            key_grad.astype(jnp.bfloat16).reshape(TOKENS, HEADS * DK),
            value_grad.astype(jnp.bfloat16).reshape(TOKENS, HEADS * DV),
            coef_parts.transpose(1, 0, 2).reshape(LEVELS, TOKENS))
```

```python
import jax
import jax.numpy as jnp
from jax import lax
from jax.experimental import pallas as pl
from jax.experimental.pallas import tpu as pltpu
from jax.sharding import PartitionSpec as P

MESH = pl.DeviceIdType.MESH
F32 = jnp.float32
BF16 = jnp.bfloat16
TOK = 1024
BLK = 128
NB = TOK // BLK
LOCAL = 11
CROSS = 6
DIAG = 8
FAR = (3, 4, 5)


def level_weight(level):
    return 1.0 if level == 0 else 2.0 ** (-(level - 1) / 2.0)


def dot(a, b):
    return jnp.dot(a, b, preferred_element_type=F32)


def dot_nt(a, b):
    return lax.dot_general(a, b, (((1,), (1,)), ((), ())), preferred_element_type=F32)


def kernel(
    q_ref, k_ref, v_ref, g_ref, lc_ref, st_ref,
    qo_ref, ko_ref, vo_ref, co_ref,
    q_t, k_t, g_t, masks, s_loc, g_loc, k_acc, v_acc,
    grads, core_in, pair_sum, l0_in, l1_in, l2_in, y_in, y_sum,
    z5_in, z4_in, z3_in, state, near, coef_all,
    core_ss, core_rs, l0_ss, l0_rs, l1_ss, l1_rs, l2_ss, l2_rs, y_ss, y_rs,
    z5_ss, z5_rs, z4_ss, z4_rs, z3_ss, z3_rs, st_ss, st_rs, nr_ss, nr_rs, x_ss, x_rs,
):
    shard = lax.axis_index("seq")
    hx = lax.axis_index("head")
    c = lax.rem(shard, 2)
    y = lax.rem(shard // 2, 4)
    z = shard // 8

    def at(cc, yy, zz):
        return ((zz * 4 + yy) * 2 + cc, hx)

    def bit(j):
        return lax.rem(shard // (1 << j), 2)

    other = 1 - c
    plane = [(cc, k) for cc in range(2) for k in range(4) if cc or k]

    def plane_dev(cc, k):
        return lax.rem(c + cc, 2), lax.rem(y + k, 4)

    barrier = pltpu.get_barrier_semaphore()
    for cc, k in plane:
        pc, py = plane_dev(cc, k)
        pl.semaphore_signal(barrier, inc=1, device_id=at(pc, py, z), device_id_type=MESH)
    for k in range(1, 8):
        pl.semaphore_signal(barrier, inc=1, device_id=at(c, y, lax.rem(z + k, 8)), device_id_type=MESH)
    for k in range(1, 4):
        pl.semaphore_signal(barrier, inc=1, device_id=(shard, lax.rem(hx + k, 4)), device_id_type=MESH)

    for h in range(2):
        hs = slice(h * BLK, (h + 1) * BLK)
        g_t[h] = g_ref[:, hs].T
        q_t[h] = q_ref[:, hs].T
        k_t[h] = k_ref[:, hs].T
    for j in reversed(range(CROSS)):
        w = level_weight(LOCAL + j)
        row = lc_ref[LOCAL + j : LOCAL + j + 1, :]
        for h in range(2):
            hs = slice(h * BLK, (h + 1) * BLK)
            scaled = (g_t[h].astype(F32) * row).astype(BF16)
            grads[j, h] = (w * dot(scaled, q_ref[:, hs])).reshape(4, 32, BLK)

    key_pos = lax.broadcasted_iota(jnp.int32, (BLK, BLK), 0)
    query_pos = lax.broadcasted_iota(jnp.int32, (BLK, BLK), 1)
    mixed = jnp.bitwise_xor(key_pos, query_pos)
    level = jnp.zeros((BLK, BLK), jnp.int32)
    for b in range(DIAG - 1):
        level = level + (mixed >= (1 << b)).astype(jnp.int32)
    for n in range(DIAG):
        hit = jnp.logical_and(level == n, key_pos <= query_pos)
        masks[n] = jnp.where(hit, level_weight(n), 0.0).astype(F32)

    for h in range(2):
        hs = slice(h * BLK, (h + 1) * BLK)
        for n in range(4):
            r = slice(n * 256, n * 256 + 128)
            s_loc[h, n] = dot(k_t[h, :, r], v_ref[r, hs]).astype(BF16)
        for n in range(2):
            r = slice(n * 512, n * 512 + 256)
            s_loc[h, 4 + n] = dot(k_t[h, :, r], v_ref[r, hs]).astype(BF16)
        s_loc[h, 6] = dot(k_t[h, :, 0:512], v_ref[0:512, hs]).astype(BF16)
    g_loc[...] = jnp.zeros_like(g_loc)

    bits = [bit(j).astype(F32) for j in range(CROSS)]

    def block(i, carry):
        ts = pl.ds(pl.multiple_of(i * BLK, BLK), BLK)
        slots = (i // 2, 4 + i // 4, 6)
        right = [lax.rem(i // (1 << n), 2).astype(F32) for n in range(3)]
        rows = [lc_ref[n : n + 1, ts] for n in range(DIAG)]
        coef = masks[0] * rows[0]
        for n in range(1, DIAG):
            coef = coef + masks[n] * rows[n]
        local = [lc_ref[DIAG + n : DIAG + n + 1, ts] * (right[n] * level_weight(DIAG + n)) for n in range(3)]
        cross = [lc_ref[LOCAL + j : LOCAL + j + 1, ts] * bits[j] for j in range(CROSS)]
        prods = None
        sums = [None] * (3 + CROSS)
        for h in range(2):
            hs = slice(h * BLK, (h + 1) * BLK)
            q_i, k_i, v_i, g_i = q_ref[ts, hs], k_ref[ts, hs], v_ref[ts, hs], g_ref[ts, hs]
            qt, kt, gt = q_t[h, :, ts], k_t[h, :, ts], g_t[h, :, ts]
            scores = dot(k_i, qt)
            grad_scores = dot(v_i, gt)
            prod = scores * grad_scores
            prods = prod if prods is None else prods + prod
            weights = (coef * scores).astype(BF16)
            grad_weights = (coef * grad_scores).astype(BF16)
            k_acc[ts, hs] = dot(grad_weights, q_i)
            v_acc[ts, hs] = dot(weights, g_i)
            acc = dot(kt, grad_weights)
            qf, gf = qt.astype(F32), gt.astype(F32)
            for n in range(3 + CROSS):
                s = s_loc[h, slots[n]] if n < 3 else st_ref[0, n - 3, h]
                projected = dot(s, gt)
                acc = acc + projected * (local[n] if n < 3 else cross[n - 3])
                part = jnp.sum(qf * projected, axis=0, keepdims=True)
                sums[n] = part if sums[n] is None else sums[n] + part
            for n in range(3):
                g_loc[h, slots[n]] += dot((gf * local[n]).astype(BF16), q_i)
            qo_ref[ts, hs] = acc.T.astype(BF16)
        for n in range(DIAG):
            coef_all[hx, n : n + 1, ts] = jnp.sum(masks[n] * prods, axis=0, keepdims=True)
        for n in range(3):
            coef_all[hx, DIAG + n : DIAG + n + 1, ts] = sums[n] * (right[n] * level_weight(DIAG + n))
        for j in range(CROSS):
            coef_all[hx, LOCAL + j : LOCAL + j + 1, ts] = sums[3 + j] * bits[j]
        return carry

    lax.fori_loop(0, NB, block, 0)

    pl.semaphore_wait(barrier, len(plane) + 7 + 3)

    sends = []

    def copy(src, dst, ss, rs, dev):
        return pltpu.make_async_remote_copy(
            src_ref=src, dst_ref=dst, send_sem=ss, recv_sem=rs, device_id=dev, device_id_type=MESH
        )

    def send(cond, *args):
        def go():
            copy(*args).start()

        def done():
            copy(*args).wait_send()

        if cond is None:
            go()
        else:
            pl.when(cond)(go)
        sends.append((cond, done))

    mate = at(other, y, z)
    for j in (5, 4, 3, 2, 1):
        send(bit(j) == 1, grads.at[j, other], core_in.at[j], core_ss.at[j], core_rs.at[j], mate)
    send(c == 1, grads.at[0], l0_in, l0_ss, l0_rs, mate)
    for k in range(1, 4):
        send(
            None, coef_all.at[hx], coef_all.at[hx], x_ss.at[k - 1], x_rs.at[k - 1],
            (shard, lax.rem(hx + k, 4)),
        )

    def y_send(n, k):
        py = lax.rem(y + k, 4)
        return (pair_sum.at[FAR[n], py], y_in.at[n, k - 1], y_ss.at[n, k - 1], y_rs.at[n, k - 1], at(c, py, z))

    for j in (5, 4, 3, 2, 1):
        on = bit(j) == 1

        @pl.when(on)
        def _():
            copy(grads.at[j, other], core_in.at[j], core_ss.at[j], core_rs.at[j], mate).wait_recv()
            pair_sum[j] = grads[j, c] + core_in[j]

        if j in FAR:
            for k in range(1, 4):
                send(on, *y_send(FAR.index(j), k))
        elif j == 2:
            for k in range(2):
                send(on, pair_sum.at[2], l2_in.at[y - 2], l2_ss.at[k], l2_rs.at[y - 2], at(c, k, z))
        else:
            send(on, pair_sum.at[1], l1_in, l1_ss, l1_rs, at(c, y - 1, z))

    z5 = lambda k: (y_sum.at[2], z5_in.at[z - 4], z5_ss.at[k], z5_rs.at[z - 4], at(c, y, k))
    z4 = lambda k: (
        y_sum.at[1], z4_in.at[lax.rem(z, 2)], z4_ss.at[k], z4_rs.at[lax.rem(z, 2)], at(c, y, (z // 4) * 4 + k)
    )
    for n in (2, 1, 0):
        on = bit(FAR[n]) == 1

        @pl.when(on)
        def _():
            total = pair_sum[FAR[n], y]
            for k in range(1, 4):
                copy(*y_send(n, k)).wait_recv()
                total = total + y_in[n, k - 1]
            y_sum[n] = total

        if n == 2:
            for k in range(4):
                send(on, *z5(k))
        elif n == 1:
            for k in range(2):
                send(on, *z4(k))
        else:
            send(on, y_sum.at[0], z3_in, z3_ss, z3_rs, at(c, y, z - 1))

    near[c] = jnp.zeros((4, 32, BLK), F32)

    @pl.when(bit(2) == 0)
    def _():
        for k in range(2):
            copy(pair_sum.at[2], l2_in.at[k], l2_ss.at[k], l2_rs.at[k], at(c, y, z)).wait_recv()
        near[c] += l2_in[0] + l2_in[1]

    @pl.when(bit(1) == 0)
    def _():
        copy(pair_sum.at[1], l1_in, l1_ss, l1_rs, at(c, y, z)).wait_recv()
        near[c] += l1_in[...]

    send(None, near.at[c], near.at[c], nr_ss, nr_rs, mate)

    for k in range(1, 4):
        px = lax.rem(hx + 4 - k, 4)
        copy(
            coef_all.at[px], coef_all.at[px], x_ss.at[k - 1], x_rs.at[k - 1], (shard, px)
        ).wait_recv()
    co_ref[...] = ((coef_all[0] + coef_all[1]) + (coef_all[2] + coef_all[3]))

    some = z < 7

    @pl.when(z == 7)
    def _():
        state[...] = jnp.zeros_like(state)

    @pl.when(some)
    def _():
        state[c, y] = jnp.zeros((32, BLK), F32)

    @pl.when(bit(3) == 0)
    def _():
        copy(y_sum.at[0], z3_in, z3_ss, z3_rs, at(c, y, z)).wait_recv()
        state[c, y] += z3_in[...]

    @pl.when(bit(4) == 0)
    def _():
        for k in range(2):
            copy(y_sum.at[1], z4_in.at[k], z4_ss.at[k], z4_rs.at[k], at(c, y, z)).wait_recv()
        state[c, y] += z4_in[0] + z4_in[1]

    @pl.when(bit(5) == 0)
    def _():
        for k in range(4):
            copy(y_sum.at[2], z5_in.at[k], z5_ss.at[k], z5_rs.at[k], at(c, y, z)).wait_recv()
        state[c, y] += (z5_in[0] + z5_in[1]) + (z5_in[2] + z5_in[3])

    for n, (cc, k) in enumerate(plane):
        pc, py = plane_dev(cc, k)
        send(some, state.at[c, y], state.at[c, y], st_ss.at[n], st_rs.at[n], at(pc, py, z))

    copy(near.at[other], near.at[other], nr_ss, nr_rs, mate).wait_recv()

    @pl.when(c == 0)
    def _():
        copy(grads.at[0], l0_in, l0_ss, l0_rs, mate).wait_recv()

    @pl.when(c == 1)
    def _():
        l0_in[...] = jnp.zeros_like(l0_in)

    @pl.when(some)
    def _():
        for n, (cc, k) in enumerate(plane):
            sc, sy = lax.rem(c + cc, 2), lax.rem(y + 4 - k, 4)
            copy(state.at[sc, sy], state.at[sc, sy], st_ss.at[n], st_rs.at[n], at(sc, sy, z)).wait_recv()

    for h in range(2):
        hs = slice(h * BLK, (h + 1) * BLK)
        base = (state[h] + (near[h] + l0_in[h])).reshape(BLK, BLK)
        for i in range(NB):
            ts = slice(i * BLK, (i + 1) * BLK)
            total = base
            for n, slot in enumerate((i // 2, 4 + i // 4, 6)):
                if (i >> n) % 2 == 0:
                    total = total + g_loc[h, slot]
            gs = total.astype(BF16)
            ko_ref[ts, hs] = (k_acc[ts, hs] + dot(v_ref[ts, hs], gs)).astype(BF16)
            vo_ref[ts, hs] = (v_acc[ts, hs] + dot_nt(k_ref[ts, hs], gs)).astype(BF16)

    for cond, done in sends:
        if cond is None:
            done()
        else:
            pl.when(cond)(done)


def shards(queries, key_vectors, values, out_grad, level_coef, saved_states):
    sem = pltpu.SemaphoreType.DMA
    quarter = (4, 32, BLK)
    vmem = pl.BlockSpec(memory_space=pltpu.VMEM)
    return tuple(
        pl.pallas_call(
            kernel,
            out_shape=[jax.ShapeDtypeStruct((TOK, 2 * BLK), BF16)] * 3
            + [jax.ShapeDtypeStruct((LOCAL + CROSS, TOK), F32)],
            in_specs=[vmem] * 6,
            out_specs=[vmem] * 4,
            scratch_shapes=[
                pltpu.VMEM((2, BLK, TOK), BF16),
                pltpu.VMEM((2, BLK, TOK), BF16),
                pltpu.VMEM((2, BLK, TOK), BF16),
                pltpu.VMEM((DIAG, BLK, BLK), F32),
                pltpu.VMEM((2, 7, BLK, BLK), BF16),
                pltpu.VMEM((2, 7, BLK, BLK), F32),
                pltpu.VMEM((TOK, 2 * BLK), F32),
                pltpu.VMEM((TOK, 2 * BLK), F32),
                pltpu.VMEM((CROSS, 2) + quarter, F32),
                pltpu.VMEM((CROSS,) + quarter, F32),
                pltpu.VMEM((CROSS,) + quarter, F32),
                pltpu.VMEM((2,) + quarter, F32),
                pltpu.VMEM(quarter, F32),
                pltpu.VMEM((2,) + quarter, F32),
                pltpu.VMEM((3, 3, 32, BLK), F32),
                pltpu.VMEM((3, 32, BLK), F32),
                pltpu.VMEM((4, 32, BLK), F32),
                pltpu.VMEM((2, 32, BLK), F32),
                pltpu.VMEM((32, BLK), F32),
                pltpu.VMEM((2,) + quarter, F32),
                pltpu.VMEM((2,) + quarter, F32),
                pltpu.VMEM((4, LOCAL + CROSS, TOK), F32),
                sem((CROSS,)), sem((CROSS,)),
                sem, sem,
                sem, sem,
                sem((2,)), sem((2,)),
                sem((3, 3)), sem((3, 3)),
                sem((4,)), sem((4,)),
                sem((2,)), sem((2,)),
                sem, sem,
                sem((7,)), sem((7,)),
                sem, sem,
                sem((3,)), sem((3,)),
            ],
            compiler_params=pltpu.CompilerParams(
                collective_id=0, has_side_effects=True, vmem_limit_bytes=40 * 2**20
            ),
        )(queries, key_vectors, values, out_grad, level_coef, saved_states)
    )


def solution(mesh):
    in_specs = (
        P("seq", "head"),
        P("seq", "head"),
        P("seq", "head"),
        P("seq", "head"),
        P(None, "seq"),
        P("seq", None, "head", None, None),
    )
    out_specs = (P("seq", "head"), P("seq", "head"), P("seq", "head"), P(None, "seq"))
    return jax.shard_map(shards, mesh=mesh, in_specs=in_specs, out_specs=out_specs, check_vma=False)
```

```python
import jax
import jax.numpy as jnp
from jax import lax
from jax.experimental import pallas as pl
from jax.experimental.pallas import tpu as pltpu
from jax.sharding import PartitionSpec as P

MESH = pl.DeviceIdType.MESH
F32 = jnp.float32
BF16 = jnp.bfloat16
TOK = 1024
BLK = 128
NB = TOK // BLK
LOCAL = 11
CROSS = 6
DIAG = 8
FAR = (3, 4, 5)


def level_weight(level):
    return 1.0 if level == 0 else 2.0 ** (-(level - 1) / 2.0)


def dot(a, b):
    return jnp.dot(a, b, preferred_element_type=F32)


def dot_nt(a, b):
    return lax.dot_general(a, b, (((1,), (1,)), ((), ())), preferred_element_type=F32)


def kernel(
    q_hbm, k_hbm, v_hbm, g_hbm, lc_hbm, st_hbm,
    qo_ref, k_ref, v_ref, k_acc, v_acc, gs_ref, co_ref,
    q_ref, g_ref, lc_ref, st_ref, load_sem,
    q_t, k_t, g_t, masks, s_loc, g_loc,
    grads, core_in, pair_sum, l0_in, l1_in, l2_in, y_in, y_sum,
    z5_in, z4_in, z3_in, state, near, coef_all,
    core_ss, core_rs, l0_ss, l0_rs, l1_ss, l1_rs, l2_ss, l2_rs, y_ss, y_rs,
    z5_ss, z5_rs, z4_ss, z4_rs, z3_ss, z3_rs, st_ss, st_rs, nr_ss, nr_rs, x_ss, x_rs,
):
    shard = lax.axis_index("seq")
    hx = lax.axis_index("head")
    c = lax.rem(shard, 2)
    y = lax.rem(shard // 2, 4)
    z = shard // 8

    def at(cc, yy, zz):
        return ((zz * 4 + yy) * 2 + cc, hx)

    def bit(j):
        return lax.rem(shard // (1 << j), 2)

    other = 1 - c
    plane = [(cc, k) for cc in range(2) for k in range(4) if cc or k]

    def plane_dev(cc, k):
        return lax.rem(c + cc, 2), lax.rem(y + k, 4)

    loads = [
        pltpu.make_async_copy(src, dst, load_sem.at[n])
        for n, (src, dst) in enumerate(
            ((g_hbm, g_ref), (lc_hbm, lc_ref), (q_hbm, q_ref), (k_hbm, k_ref), (v_hbm, v_ref), (st_hbm, st_ref))
        )
    ]
    for load in loads:
        load.start()

    barrier = pltpu.get_barrier_semaphore()
    for cc, k in plane:
        pc, py = plane_dev(cc, k)
        pl.semaphore_signal(barrier, inc=1, device_id=at(pc, py, z), device_id_type=MESH)
    for k in range(1, 8):
        pl.semaphore_signal(barrier, inc=1, device_id=at(c, y, lax.rem(z + k, 8)), device_id_type=MESH)
    for k in range(1, 4):
        pl.semaphore_signal(barrier, inc=1, device_id=(shard, lax.rem(hx + k, 4)), device_id_type=MESH)

    for n in range(3):
        loads[n].wait()
    for h in range(2):
        hs = slice(h * BLK, (h + 1) * BLK)
        g_t[h] = g_ref[:, hs].T
    for j in reversed(range(CROSS)):
        w = level_weight(LOCAL + j)
        row = lc_ref[LOCAL + j : LOCAL + j + 1, :]
        for h in range(2):
            hs = slice(h * BLK, (h + 1) * BLK)
            scaled = (g_t[h].astype(F32) * row).astype(BF16)
            grads[j, h] = (w * dot(scaled, q_ref[:, hs])).reshape(4, 32, BLK)

    key_pos = lax.broadcasted_iota(jnp.int32, (BLK, BLK), 0)
    query_pos = lax.broadcasted_iota(jnp.int32, (BLK, BLK), 1)
    mixed = jnp.bitwise_xor(key_pos, query_pos)
    level = jnp.zeros((BLK, BLK), jnp.int32)
    for b in range(DIAG - 1):
        level = level + (mixed >= (1 << b)).astype(jnp.int32)
    for n in range(DIAG):
        hit = jnp.logical_and(level == n, key_pos <= query_pos)
        masks[n] = jnp.where(hit, level_weight(n), 0.0).astype(F32)

    for n in range(3, 6):
        loads[n].wait()
    for h in range(2):
        hs = slice(h * BLK, (h + 1) * BLK)
        q_t[h] = q_ref[:, hs].T
        k_t[h] = k_ref[:, hs].T

    for h in range(2):
        hs = slice(h * BLK, (h + 1) * BLK)
        for n in range(4):
            r = slice(n * 256, n * 256 + 128)
            s_loc[h, n] = dot(k_t[h, :, r], v_ref[r, hs]).astype(BF16)
        for n in range(2):
            r = slice(n * 512, n * 512 + 256)
            s_loc[h, 4 + n] = dot(k_t[h, :, r], v_ref[r, hs]).astype(BF16)
        s_loc[h, 6] = dot(k_t[h, :, 0:512], v_ref[0:512, hs]).astype(BF16)
    g_loc[...] = jnp.zeros_like(g_loc)

    bits = [bit(j).astype(F32) for j in range(CROSS)]

    def block(i, carry):
        ts = pl.ds(pl.multiple_of(i * BLK, BLK), BLK)
        slots = (i // 2, 4 + i // 4, 6)
        right = [lax.rem(i // (1 << n), 2).astype(F32) for n in range(3)]
        rows = [lc_ref[n : n + 1, ts] for n in range(DIAG)]
        coef = masks[0] * rows[0]
        for n in range(1, DIAG):
            coef = coef + masks[n] * rows[n]
        local = [lc_ref[DIAG + n : DIAG + n + 1, ts] * (right[n] * level_weight(DIAG + n)) for n in range(3)]
        cross = [lc_ref[LOCAL + j : LOCAL + j + 1, ts] * bits[j] for j in range(CROSS)]
        prods = None
        sums = [None] * (3 + CROSS)
        for h in range(2):
            hs = slice(h * BLK, (h + 1) * BLK)
            q_i, k_i, v_i, g_i = q_ref[ts, hs], k_ref[ts, hs], v_ref[ts, hs], g_ref[ts, hs]
            qt, kt, gt = q_t[h, :, ts], k_t[h, :, ts], g_t[h, :, ts]
            scores = dot(k_i, qt)
            grad_scores = dot(v_i, gt)
            prod = scores * grad_scores
            prods = prod if prods is None else prods + prod
            weights = (coef * scores).astype(BF16)
            grad_weights = (coef * grad_scores).astype(BF16)
            k_acc[ts, hs] = dot(grad_weights, q_i)
            v_acc[ts, hs] = dot(weights, g_i)
            acc = dot(kt, grad_weights)
            qf, gf = qt.astype(F32), gt.astype(F32)
            for n in range(3 + CROSS):
                s = s_loc[h, slots[n]] if n < 3 else st_ref[0, n - 3, h]
                projected = dot(s, gt)
                acc = acc + projected * (local[n] if n < 3 else cross[n - 3])
                part = jnp.sum(qf * projected, axis=0, keepdims=True)
                sums[n] = part if sums[n] is None else sums[n] + part
            for n in range(3):
                g_loc[h, slots[n]] += dot((gf * local[n]).astype(BF16), q_i)
            qo_ref[ts, hs] = acc.T.astype(BF16)
        for n in range(DIAG):
            coef_all[hx, n : n + 1, ts] = jnp.sum(masks[n] * prods, axis=0, keepdims=True)
        for n in range(3):
            coef_all[hx, DIAG + n : DIAG + n + 1, ts] = sums[n] * (right[n] * level_weight(DIAG + n))
        for j in range(CROSS):
            coef_all[hx, LOCAL + j : LOCAL + j + 1, ts] = sums[3 + j] * bits[j]
        return carry

    lax.fori_loop(0, NB, block, 0)

    pl.semaphore_wait(barrier, len(plane) + 7 + 3)

    sends = []

    def copy(src, dst, ss, rs, dev):
        return pltpu.make_async_remote_copy(
            src_ref=src, dst_ref=dst, send_sem=ss, recv_sem=rs, device_id=dev, device_id_type=MESH
        )

    def send(cond, *args):
        def go():
            copy(*args).start()

        def done():
            copy(*args).wait_send()

        if cond is None:
            go()
        else:
            pl.when(cond)(go)
        sends.append((cond, done))

    mate = at(other, y, z)
    for j in (5, 4, 3, 2, 1):
        send(bit(j) == 1, grads.at[j, other], core_in.at[j], core_ss.at[j], core_rs.at[j], mate)
    send(c == 1, grads.at[0], l0_in, l0_ss, l0_rs, mate)
    for k in range(1, 4):
        send(
            None, coef_all.at[hx], coef_all.at[hx], x_ss.at[k - 1], x_rs.at[k - 1],
            (shard, lax.rem(hx + k, 4)),
        )

    def y_send(n, k):
        py = lax.rem(y + k, 4)
        return (pair_sum.at[FAR[n], py], y_in.at[n, k - 1], y_ss.at[n, k - 1], y_rs.at[n, k - 1], at(c, py, z))

    for j in (5, 4, 3, 2, 1):
        on = bit(j) == 1

        @pl.when(on)
        def _():
            copy(grads.at[j, other], core_in.at[j], core_ss.at[j], core_rs.at[j], mate).wait_recv()
            pair_sum[j] = grads[j, c] + core_in[j]

        if j in FAR:
            for k in range(1, 4):
                send(on, *y_send(FAR.index(j), k))
        elif j == 2:
            for k in range(2):
                send(on, pair_sum.at[2], l2_in.at[y - 2], l2_ss.at[k], l2_rs.at[y - 2], at(c, k, z))
        else:
            send(on, pair_sum.at[1], l1_in, l1_ss, l1_rs, at(c, y - 1, z))

    z5 = lambda k: (y_sum.at[2], z5_in.at[z - 4], z5_ss.at[k], z5_rs.at[z - 4], at(c, y, k))
    z4 = lambda k: (
        y_sum.at[1], z4_in.at[lax.rem(z, 2)], z4_ss.at[k], z4_rs.at[lax.rem(z, 2)], at(c, y, (z // 4) * 4 + k)
    )
    for n in (2, 1, 0):
        on = bit(FAR[n]) == 1

        @pl.when(on)
        def _():
            total = pair_sum[FAR[n], y]
            for k in range(1, 4):
                copy(*y_send(n, k)).wait_recv()
                total = total + y_in[n, k - 1]
            y_sum[n] = total

        if n == 2:
            for k in range(4):
                send(on, *z5(k))
        elif n == 1:
            for k in range(2):
                send(on, *z4(k))
        else:
            send(on, y_sum.at[0], z3_in, z3_ss, z3_rs, at(c, y, z - 1))

    near[c] = jnp.zeros((4, 32, BLK), F32)

    @pl.when(bit(2) == 0)
    def _():
        for k in range(2):
            copy(pair_sum.at[2], l2_in.at[k], l2_ss.at[k], l2_rs.at[k], at(c, y, z)).wait_recv()
        near[c] += l2_in[0] + l2_in[1]

    @pl.when(bit(1) == 0)
    def _():
        copy(pair_sum.at[1], l1_in, l1_ss, l1_rs, at(c, y, z)).wait_recv()
        near[c] += l1_in[...]

    send(None, near.at[c], near.at[c], nr_ss, nr_rs, mate)

    for k in range(1, 4):
        px = lax.rem(hx + 4 - k, 4)
        copy(
            coef_all.at[px], coef_all.at[px], x_ss.at[k - 1], x_rs.at[k - 1], (shard, px)
        ).wait_recv()
    co_ref[...] = ((coef_all[0] + coef_all[1]) + (coef_all[2] + coef_all[3]))

    some = z < 7

    @pl.when(z == 7)
    def _():
        state[...] = jnp.zeros_like(state)

    @pl.when(some)
    def _():
        state[c, y] = jnp.zeros((32, BLK), F32)

    @pl.when(bit(3) == 0)
    def _():
        copy(y_sum.at[0], z3_in, z3_ss, z3_rs, at(c, y, z)).wait_recv()
        state[c, y] += z3_in[...]

    @pl.when(bit(4) == 0)
    def _():
        for k in range(2):
            copy(y_sum.at[1], z4_in.at[k], z4_ss.at[k], z4_rs.at[k], at(c, y, z)).wait_recv()
        state[c, y] += z4_in[0] + z4_in[1]

    @pl.when(bit(5) == 0)
    def _():
        for k in range(4):
            copy(y_sum.at[2], z5_in.at[k], z5_ss.at[k], z5_rs.at[k], at(c, y, z)).wait_recv()
        state[c, y] += (z5_in[0] + z5_in[1]) + (z5_in[2] + z5_in[3])

    for n, (cc, k) in enumerate(plane):
        pc, py = plane_dev(cc, k)
        send(some, state.at[c, y], state.at[c, y], st_ss.at[n], st_rs.at[n], at(pc, py, z))

    copy(near.at[other], near.at[other], nr_ss, nr_rs, mate).wait_recv()

    @pl.when(c == 0)
    def _():
        copy(grads.at[0], l0_in, l0_ss, l0_rs, mate).wait_recv()

    @pl.when(c == 1)
    def _():
        l0_in[...] = jnp.zeros_like(l0_in)

    @pl.when(some)
    def _():
        for n, (cc, k) in enumerate(plane):
            sc, sy = lax.rem(c + cc, 2), lax.rem(y + 4 - k, 4)
            copy(state.at[sc, sy], state.at[sc, sy], st_ss.at[n], st_rs.at[n], at(sc, sy, z)).wait_recv()

    for h in range(2):
        base = (state[h] + (near[h] + l0_in[h])).reshape(BLK, BLK)
        for i in range(NB):
            total = base
            for n, slot in enumerate((i // 2, 4 + i // 4, 6)):
                if (i >> n) % 2 == 0:
                    total = total + g_loc[h, slot]
            gs_ref[h, i] = total.astype(BF16)

    for cond, done in sends:
        if cond is None:
            done()
        else:
            pl.when(cond)(done)


def finish(
    qi_ref, k_ref, v_ref, k_acc, v_acc, gs_ref, ci_ref,
    qo_hbm, ko_hbm, vo_hbm, co_hbm,
    ko, vo, sem,
):
    writes = [
        pltpu.make_async_copy(qi_ref, qo_hbm, sem.at[0]),
        pltpu.make_async_copy(ci_ref, co_hbm, sem.at[1]),
    ]
    for write in writes:
        write.start()
    for i in range(NB):
        ts = slice(i * BLK, (i + 1) * BLK)
        for h in range(2):
            hs = slice(h * BLK, (h + 1) * BLK)
            gs = gs_ref[h, i]
            ko[ts, hs] = (k_acc[ts, hs] + dot(v_ref[ts, hs], gs)).astype(BF16)
            vo[ts, hs] = (v_acc[ts, hs] + dot_nt(k_ref[ts, hs], gs)).astype(BF16)
        for n, (src, dst) in enumerate(((ko, ko_hbm), (vo, vo_hbm))):
            write = pltpu.make_async_copy(src.at[ts], dst.at[ts], sem.at[2 + 2 * i + n])
            write.start()
            writes.append(write)
    for write in writes:
        write.wait()


def shards(queries, key_vectors, values, out_grad, level_coef, saved_states):
    sem = pltpu.SemaphoreType.DMA
    quarter = (4, 32, BLK)
    vmem = pl.BlockSpec(memory_space=pltpu.VMEM)
    hbm = pl.BlockSpec(memory_space=pltpu.HBM)
    tokens = jax.ShapeDtypeStruct((TOK, 2 * BLK), BF16)
    sums = jax.ShapeDtypeStruct((TOK, 2 * BLK), F32)
    coefs = jax.ShapeDtypeStruct((LOCAL + CROSS, TOK), F32)
    parts = pl.pallas_call(
            kernel,
            out_shape=[tokens] * 3 + [sums] * 2 + [jax.ShapeDtypeStruct((2, NB, BLK, BLK), BF16), coefs],
            in_specs=[hbm] * 6,
            out_specs=[vmem] * 7,
            scratch_shapes=[
                pltpu.VMEM((TOK, 2 * BLK), BF16),
                pltpu.VMEM((TOK, 2 * BLK), BF16),
                pltpu.VMEM((LOCAL + CROSS, TOK), F32),
                pltpu.VMEM((1, CROSS, 2, BLK, BLK), BF16),
                sem((6,)),
                pltpu.VMEM((2, BLK, TOK), BF16),
                pltpu.VMEM((2, BLK, TOK), BF16),
                pltpu.VMEM((2, BLK, TOK), BF16),
                pltpu.VMEM((DIAG, BLK, BLK), F32),
                pltpu.VMEM((2, 7, BLK, BLK), BF16),
                pltpu.VMEM((2, 7, BLK, BLK), F32),
                pltpu.VMEM((CROSS, 2) + quarter, F32),
                pltpu.VMEM((CROSS,) + quarter, F32),
                pltpu.VMEM((CROSS,) + quarter, F32),
                pltpu.VMEM((2,) + quarter, F32),
                pltpu.VMEM(quarter, F32),
                pltpu.VMEM((2,) + quarter, F32),
                pltpu.VMEM((3, 3, 32, BLK), F32),
                pltpu.VMEM((3, 32, BLK), F32),
                pltpu.VMEM((4, 32, BLK), F32),
                pltpu.VMEM((2, 32, BLK), F32),
                pltpu.VMEM((32, BLK), F32),
                pltpu.VMEM((2,) + quarter, F32),
                pltpu.VMEM((2,) + quarter, F32),
                pltpu.VMEM((4, LOCAL + CROSS, TOK), F32),
                sem((CROSS,)), sem((CROSS,)),
                sem, sem,
                sem, sem,
                sem((2,)), sem((2,)),
                sem((3, 3)), sem((3, 3)),
                sem((4,)), sem((4,)),
                sem((2,)), sem((2,)),
                sem, sem,
                sem((7,)), sem((7,)),
                sem, sem,
                sem((3,)), sem((3,)),
            ],
            compiler_params=pltpu.CompilerParams(
                collective_id=0, has_side_effects=True, vmem_limit_bytes=40 * 2**20
            ),
        )(*[pltpu.with_memory_space_constraint(a, pltpu.HBM) for a in (queries, key_vectors, values, out_grad, level_coef, saved_states)])
    return tuple(
        pl.pallas_call(
            finish,
            out_shape=[tokens] * 3 + [coefs],
            in_specs=[vmem] * 7,
            out_specs=[hbm] * 4,
            scratch_shapes=[
                pltpu.VMEM((TOK, 2 * BLK), BF16),
                pltpu.VMEM((TOK, 2 * BLK), BF16),
                sem((2 + 2 * NB,)),
            ],
            compiler_params=pltpu.CompilerParams(vmem_limit_bytes=16 * 2**20),
        )(*parts)
    )


def solution(mesh):
    in_specs = (
        P("seq", "head"),
        P("seq", "head"),
        P("seq", "head"),
        P("seq", "head"),
        P(None, "seq"),
        P("seq", None, "head", None, None),
    )
    out_specs = (P("seq", "head"), P("seq", "head"), P("seq", "head"), P(None, "seq"))
    return jax.shard_map(shards, mesh=mesh, in_specs=in_specs, out_specs=out_specs, check_vma=False)
```

```python
import jax
import jax.numpy as jnp
from jax import lax
from jax.experimental import pallas as pl
from jax.experimental.pallas import tpu as pltpu
from jax.sharding import PartitionSpec as P

MESH = pl.DeviceIdType.MESH
F32 = jnp.float32
BF16 = jnp.bfloat16
TOK = 1024
BLK = 128
NB = TOK // BLK
LOCAL = 11
CROSS = 6
DIAG = 8
FAR = (3, 4, 5)


def level_weight(level):
    return 1.0 if level == 0 else 2.0 ** (-(level - 1) / 2.0)


def dot(a, b):
    return jnp.dot(a, b, preferred_element_type=F32)


def dot_nt(a, b):
    return lax.dot_general(a, b, (((1,), (1,)), ((), ())), preferred_element_type=F32)


def kernel(
    q_hbm, k_hbm, v_hbm, g_hbm, lc_hbm, st_hbm,
    qo_ref, k_ref, v_ref, k_acc, v_acc, gs_ref, co_ref,
    q_ref, g_ref, lc_ref, st_ref, load_sem,
    q_t, k_t, g_t, masks, s_loc, g_loc,
    grads, core_in, pair_sum, l0_in, l1_in, l2_in, y_in, y_sum,
    z5_in, z4_in, z3_in, state, near, coef_all,
    relay_sem, core_ss, core_rs, l0_ss, l0_rs, l1_ss, l1_rs, l2_ss, l2_rs, y_ss, y_rs,
    z5_ss, z5_rs, z4_ss, z4_rs, z3_ss, z3_rs, st_ss, st_rs, nr_ss, nr_rs, x_ss, x_rs,
):
    shard = lax.axis_index("seq")
    hx = lax.axis_index("head")
    c = lax.rem(shard, 2)
    y = lax.rem(shard // 2, 4)
    z = shard // 8

    def at(cc, yy, zz):
        return ((zz * 4 + yy) * 2 + cc, hx)

    def bit(j):
        return lax.rem(shard // (1 << j), 2)

    other = 1 - c
    plane = [(cc, k) for cc in range(2) for k in range(4) if cc or k]

    def plane_dev(cc, k):
        return lax.rem(c + cc, 2), lax.rem(y + k, 4)

    loads = [
        pltpu.make_async_copy(src, dst, load_sem.at[n])
        for n, (src, dst) in enumerate(
            ((g_hbm, g_ref), (lc_hbm, lc_ref), (q_hbm, q_ref), (k_hbm, k_ref), (v_hbm, v_ref), (st_hbm, st_ref))
        )
    ]
    for load in loads:
        load.start()

    barrier = pltpu.get_barrier_semaphore()
    for cc, k in plane:
        pc, py = plane_dev(cc, k)
        pl.semaphore_signal(barrier, inc=1, device_id=at(pc, py, z), device_id_type=MESH)
    for k in (1, 7):
        pl.semaphore_signal(barrier, inc=1, device_id=at(c, y, lax.rem(z + k, 8)), device_id_type=MESH)
    for k in range(1, 4):
        pl.semaphore_signal(barrier, inc=1, device_id=(shard, lax.rem(hx + k, 4)), device_id_type=MESH)

    for n in range(3):
        loads[n].wait()
    for h in range(2):
        hs = slice(h * BLK, (h + 1) * BLK)
        g_t[h] = g_ref[:, hs].T
    for j in reversed(range(CROSS)):
        w = level_weight(LOCAL + j)
        row = lc_ref[LOCAL + j : LOCAL + j + 1, :]
        for h in range(2):
            hs = slice(h * BLK, (h + 1) * BLK)
            scaled = (g_t[h].astype(F32) * row).astype(BF16)
            grads[j, h] = (w * dot(scaled, q_ref[:, hs])).reshape(4, 32, BLK)

    key_pos = lax.broadcasted_iota(jnp.int32, (BLK, BLK), 0)
    query_pos = lax.broadcasted_iota(jnp.int32, (BLK, BLK), 1)
    mixed = jnp.bitwise_xor(key_pos, query_pos)
    level = jnp.zeros((BLK, BLK), jnp.int32)
    for b in range(DIAG - 1):
        level = level + (mixed >= (1 << b)).astype(jnp.int32)
    for n in range(DIAG):
        hit = jnp.logical_and(level == n, key_pos <= query_pos)
        masks[n] = jnp.where(hit, level_weight(n), 0.0).astype(F32)

    for n in range(3, 6):
        loads[n].wait()
    for h in range(2):
        hs = slice(h * BLK, (h + 1) * BLK)
        q_t[h] = q_ref[:, hs].T
        k_t[h] = k_ref[:, hs].T

    for h in range(2):
        hs = slice(h * BLK, (h + 1) * BLK)
        for n in range(4):
            r = slice(n * 256, n * 256 + 128)
            s_loc[h, n] = dot(k_t[h, :, r], v_ref[r, hs]).astype(BF16)
        for n in range(2):
            r = slice(n * 512, n * 512 + 256)
            s_loc[h, 4 + n] = dot(k_t[h, :, r], v_ref[r, hs]).astype(BF16)
        s_loc[h, 6] = dot(k_t[h, :, 0:512], v_ref[0:512, hs]).astype(BF16)
    g_loc[...] = jnp.zeros_like(g_loc)

    bits = [bit(j).astype(F32) for j in range(CROSS)]

    def block(i, carry):
        ts = pl.ds(pl.multiple_of(i * BLK, BLK), BLK)
        slots = (i // 2, 4 + i // 4, 6)
        right = [lax.rem(i // (1 << n), 2).astype(F32) for n in range(3)]
        rows = [lc_ref[n : n + 1, ts] for n in range(DIAG)]
        coef = masks[0] * rows[0]
        for n in range(1, DIAG):
            coef = coef + masks[n] * rows[n]
        local = [lc_ref[DIAG + n : DIAG + n + 1, ts] * (right[n] * level_weight(DIAG + n)) for n in range(3)]
        cross = [lc_ref[LOCAL + j : LOCAL + j + 1, ts] * bits[j] for j in range(CROSS)]
        prods = None
        sums = [None] * (3 + CROSS)
        for h in range(2):
            hs = slice(h * BLK, (h + 1) * BLK)
            q_i, k_i, v_i, g_i = q_ref[ts, hs], k_ref[ts, hs], v_ref[ts, hs], g_ref[ts, hs]
            qt, kt, gt = q_t[h, :, ts], k_t[h, :, ts], g_t[h, :, ts]
            scores = dot(k_i, qt)
            grad_scores = dot(v_i, gt)
            prod = scores * grad_scores
            prods = prod if prods is None else prods + prod
            weights = (coef * scores).astype(BF16)
            grad_weights = (coef * grad_scores).astype(BF16)
            k_acc[ts, hs] = dot(grad_weights, q_i)
            v_acc[ts, hs] = dot(weights, g_i)
            acc = dot(kt, grad_weights)
            qf, gf = qt.astype(F32), gt.astype(F32)
            for n in range(3 + CROSS):
                s = s_loc[h, slots[n]] if n < 3 else st_ref[0, n - 3, h]
                projected = dot(s, gt)
                acc = acc + projected * (local[n] if n < 3 else cross[n - 3])
                part = jnp.sum(qf * projected, axis=0, keepdims=True)
                sums[n] = part if sums[n] is None else sums[n] + part
            for n in range(3):
                g_loc[h, slots[n]] += dot((gf * local[n]).astype(BF16), q_i)
            qo_ref[ts, hs] = acc.T.astype(BF16)
        for n in range(DIAG):
            coef_all[hx, n : n + 1, ts] = jnp.sum(masks[n] * prods, axis=0, keepdims=True)
        for n in range(3):
            coef_all[hx, DIAG + n : DIAG + n + 1, ts] = sums[n] * (right[n] * level_weight(DIAG + n))
        for j in range(CROSS):
            coef_all[hx, LOCAL + j : LOCAL + j + 1, ts] = sums[3 + j] * bits[j]
        return carry

    pl.semaphore_wait(barrier, len(plane) + 2 + 3)

    def relay(step):
        far = 1 << step
        for way, k in enumerate((far, 8 - far)):
            pl.semaphore_signal(
                relay_sem.at[step, way], inc=1, device_id=at(c, y, lax.rem(z + k, 8)), device_id_type=MESH
            )

    def relayed(step):
        for way in range(2):
            pl.semaphore_wait(relay_sem.at[step, way], 1)

    relay(0)

    sends = []

    def copy(src, dst, ss, rs, dev):
        return pltpu.make_async_remote_copy(
            src_ref=src, dst_ref=dst, send_sem=ss, recv_sem=rs, device_id=dev, device_id_type=MESH
        )

    def send(cond, *args):
        def go():
            copy(*args).start()

        def done():
            copy(*args).wait_send()

        if cond is None:
            go()
        else:
            pl.when(cond)(go)
        sends.append((cond, done))

    mate = at(other, y, z)
    for j in (5, 4, 3, 2, 1):
        send(bit(j) == 1, grads.at[j, other], core_in.at[j], core_ss.at[j], core_rs.at[j], mate)
    send(c == 1, grads.at[0], l0_in, l0_ss, l0_rs, mate)
    relayed(0)
    relay(1)

    def y_send(n, k):
        py = lax.rem(y + k, 4)
        return (pair_sum.at[FAR[n], py], y_in.at[n, k - 1], y_ss.at[n, k - 1], y_rs.at[n, k - 1], at(c, py, z))

    for j in (5, 4, 3, 2, 1):
        on = bit(j) == 1

        @pl.when(on)
        def _():
            copy(grads.at[j, other], core_in.at[j], core_ss.at[j], core_rs.at[j], mate).wait_recv()
            pair_sum[j] = grads[j, c] + core_in[j]

        if j in FAR:
            for k in range(1, 4):
                send(on, *y_send(FAR.index(j), k))

    lax.fori_loop(0, NB // 2, block, 0)

    z5 = lambda k: (y_sum.at[2], z5_in.at[z - 4], z5_ss.at[k], z5_rs.at[z - 4], at(c, y, k))
    relayed(1)
    z4 = lambda k: (
        y_sum.at[1], z4_in.at[lax.rem(z, 2)], z4_ss.at[k], z4_rs.at[lax.rem(z, 2)], at(c, y, (z // 4) * 4 + k)
    )
    for n in (2, 1, 0):
        on = bit(FAR[n]) == 1

        @pl.when(on)
        def _():
            total = pair_sum[FAR[n], y]
            for k in range(1, 4):
                copy(*y_send(n, k)).wait_recv()
                total = total + y_in[n, k - 1]
            y_sum[n] = total

        if n == 2:
            for k in range(4):
                send(on, *z5(k))
        elif n == 1:
            for k in range(2):
                send(on, *z4(k))
        else:
            send(on, y_sum.at[0], z3_in, z3_ss, z3_rs, at(c, y, z - 1))

    for k in range(2):
        send(bit(2) == 1, pair_sum.at[2], l2_in.at[y - 2], l2_ss.at[k], l2_rs.at[y - 2], at(c, k, z))
    send(bit(1) == 1, pair_sum.at[1], l1_in, l1_ss, l1_rs, at(c, y - 1, z))

    lax.fori_loop(NB // 2, NB, block, 0)

    for k in range(1, 4):
        send(
            None, coef_all.at[hx], coef_all.at[hx], x_ss.at[k - 1], x_rs.at[k - 1],
            (shard, lax.rem(hx + k, 4)),
        )

    near[c] = jnp.zeros((4, 32, BLK), F32)

    @pl.when(bit(2) == 0)
    def _():
        for k in range(2):
            copy(pair_sum.at[2], l2_in.at[k], l2_ss.at[k], l2_rs.at[k], at(c, y, z)).wait_recv()
        near[c] += l2_in[0] + l2_in[1]

    @pl.when(bit(1) == 0)
    def _():
        copy(pair_sum.at[1], l1_in, l1_ss, l1_rs, at(c, y, z)).wait_recv()
        near[c] += l1_in[...]

    send(None, near.at[c], near.at[c], nr_ss, nr_rs, mate)

    some = z < 7

    @pl.when(z == 7)
    def _():
        state[...] = jnp.zeros_like(state)

    @pl.when(some)
    def _():
        state[c, y] = jnp.zeros((32, BLK), F32)

    @pl.when(bit(3) == 0)
    def _():
        copy(y_sum.at[0], z3_in, z3_ss, z3_rs, at(c, y, z)).wait_recv()
        state[c, y] += z3_in[...]

    @pl.when(bit(4) == 0)
    def _():
        for k in range(2):
            copy(y_sum.at[1], z4_in.at[k], z4_ss.at[k], z4_rs.at[k], at(c, y, z)).wait_recv()
        state[c, y] += z4_in[0] + z4_in[1]

    @pl.when(bit(5) == 0)
    def _():
        for k in range(4):
            copy(y_sum.at[2], z5_in.at[k], z5_ss.at[k], z5_rs.at[k], at(c, y, z)).wait_recv()
        state[c, y] += (z5_in[0] + z5_in[1]) + (z5_in[2] + z5_in[3])

    for n, (cc, k) in enumerate(plane):
        pc, py = plane_dev(cc, k)
        send(some, state.at[c, y], state.at[c, y], st_ss.at[n], st_rs.at[n], at(pc, py, z))

    for k in range(1, 4):
        px = lax.rem(hx + 4 - k, 4)
        copy(
            coef_all.at[px], coef_all.at[px], x_ss.at[k - 1], x_rs.at[k - 1], (shard, px)
        ).wait_recv()
    co_ref[...] = ((coef_all[0] + coef_all[1]) + (coef_all[2] + coef_all[3]))

    copy(near.at[other], near.at[other], nr_ss, nr_rs, mate).wait_recv()

    @pl.when(c == 0)
    def _():
        copy(grads.at[0], l0_in, l0_ss, l0_rs, mate).wait_recv()

    @pl.when(c == 1)
    def _():
        l0_in[...] = jnp.zeros_like(l0_in)

    @pl.when(some)
    def _():
        for n, (cc, k) in enumerate(plane):
            sc, sy = lax.rem(c + cc, 2), lax.rem(y + 4 - k, 4)
            copy(state.at[sc, sy], state.at[sc, sy], st_ss.at[n], st_rs.at[n], at(sc, sy, z)).wait_recv()

    for h in range(2):
        base = (state[h] + (near[h] + l0_in[h])).reshape(BLK, BLK)
        for i in range(NB):
            total = base
            for n, slot in enumerate((i // 2, 4 + i // 4, 6)):
                if (i >> n) % 2 == 0:
                    total = total + g_loc[h, slot]
            gs_ref[h, i] = total.astype(BF16)

    for cond, done in sends:
        if cond is None:
            done()
        else:
            pl.when(cond)(done)


def finish(
    qi_ref, k_ref, v_ref, k_acc, v_acc, gs_ref, ci_ref,
    qo_hbm, ko_hbm, vo_hbm, co_hbm,
    ko, vo, sem,
):
    writes = [
        pltpu.make_async_copy(qi_ref, qo_hbm, sem.at[0]),
        pltpu.make_async_copy(ci_ref, co_hbm, sem.at[1]),
    ]
    for write in writes:
        write.start()
    for i in range(NB):
        ts = slice(i * BLK, (i + 1) * BLK)
        for h in range(2):
            hs = slice(h * BLK, (h + 1) * BLK)
            gs = gs_ref[h, i]
            ko[ts, hs] = (k_acc[ts, hs] + dot(v_ref[ts, hs], gs)).astype(BF16)
            vo[ts, hs] = (v_acc[ts, hs] + dot_nt(k_ref[ts, hs], gs)).astype(BF16)
        for n, (src, dst) in enumerate(((ko, ko_hbm), (vo, vo_hbm))):
            write = pltpu.make_async_copy(src.at[ts], dst.at[ts], sem.at[2 + 2 * i + n])
            write.start()
            writes.append(write)
    for write in writes:
        write.wait()


def shards(queries, key_vectors, values, out_grad, level_coef, saved_states):
    sem = pltpu.SemaphoreType.DMA
    quarter = (4, 32, BLK)
    vmem = pl.BlockSpec(memory_space=pltpu.VMEM)
    hbm = pl.BlockSpec(memory_space=pltpu.HBM)
    tokens = jax.ShapeDtypeStruct((TOK, 2 * BLK), BF16)
    sums = jax.ShapeDtypeStruct((TOK, 2 * BLK), F32)
    coefs = jax.ShapeDtypeStruct((LOCAL + CROSS, TOK), F32)
    parts = pl.pallas_call(
            kernel,
            out_shape=[tokens] * 3 + [sums] * 2 + [jax.ShapeDtypeStruct((2, NB, BLK, BLK), BF16), coefs],
            in_specs=[hbm] * 6,
            out_specs=[vmem] * 7,
            scratch_shapes=[
                pltpu.VMEM((TOK, 2 * BLK), BF16),
                pltpu.VMEM((TOK, 2 * BLK), BF16),
                pltpu.VMEM((LOCAL + CROSS, TOK), F32),
                pltpu.VMEM((1, CROSS, 2, BLK, BLK), BF16),
                sem((6,)),
                pltpu.VMEM((2, BLK, TOK), BF16),
                pltpu.VMEM((2, BLK, TOK), BF16),
                pltpu.VMEM((2, BLK, TOK), BF16),
                pltpu.VMEM((DIAG, BLK, BLK), F32),
                pltpu.VMEM((2, 7, BLK, BLK), BF16),
                pltpu.VMEM((2, 7, BLK, BLK), F32),
                pltpu.VMEM((CROSS, 2) + quarter, F32),
                pltpu.VMEM((CROSS,) + quarter, F32),
                pltpu.VMEM((CROSS,) + quarter, F32),
                pltpu.VMEM((2,) + quarter, F32),
                pltpu.VMEM(quarter, F32),
                pltpu.VMEM((2,) + quarter, F32),
                pltpu.VMEM((3, 3, 32, BLK), F32),
                pltpu.VMEM((3, 32, BLK), F32),
                pltpu.VMEM((4, 32, BLK), F32),
                pltpu.VMEM((2, 32, BLK), F32),
                pltpu.VMEM((32, BLK), F32),
                pltpu.VMEM((2,) + quarter, F32),
                pltpu.VMEM((2,) + quarter, F32),
                pltpu.VMEM((4, LOCAL + CROSS, TOK), F32),
                pltpu.SemaphoreType.REGULAR((2, 2)),
                sem((CROSS,)), sem((CROSS,)),
                sem, sem,
                sem, sem,
                sem((2,)), sem((2,)),
                sem((3, 3)), sem((3, 3)),
                sem((4,)), sem((4,)),
                sem((2,)), sem((2,)),
                sem, sem,
                sem((7,)), sem((7,)),
                sem, sem,
                sem((3,)), sem((3,)),
            ],
            compiler_params=pltpu.CompilerParams(
                collective_id=0, has_side_effects=True, vmem_limit_bytes=40 * 2**20
            ),
        )(*[pltpu.with_memory_space_constraint(a, pltpu.HBM) for a in (queries, key_vectors, values, out_grad, level_coef, saved_states)])
    return tuple(
        pl.pallas_call(
            finish,
            out_shape=[tokens] * 3 + [coefs],
            in_specs=[vmem] * 7,
            out_specs=[hbm] * 4,
            scratch_shapes=[
                pltpu.VMEM((TOK, 2 * BLK), BF16),
                pltpu.VMEM((TOK, 2 * BLK), BF16),
                sem((2 + 2 * NB,)),
            ],
            compiler_params=pltpu.CompilerParams(vmem_limit_bytes=16 * 2**20),
        )(*parts)
    )


def solution(mesh):
    in_specs = (
        P("seq", "head"),
        P("seq", "head"),
        P("seq", "head"),
        P("seq", "head"),
        P(None, "seq"),
        P("seq", None, "head", None, None),
    )
    out_specs = (P("seq", "head"), P("seq", "head"), P("seq", "head"), P(None, "seq"))
    return jax.shard_map(shards, mesh=mesh, in_specs=in_specs, out_specs=out_specs, check_vma=False)
```

```python
import jax
import jax.numpy as jnp
from jax import lax
from jax.experimental import pallas as pl
from jax.experimental.pallas import tpu as pltpu
from jax.sharding import PartitionSpec as P

MESH = pl.DeviceIdType.MESH
F32 = jnp.float32
BF16 = jnp.bfloat16
TOK = 1024
BLK = 128
NB = TOK // BLK
LOCAL = 11
CROSS = 6
DIAG = 8
FAR = (3, 4, 5)


def level_weight(level):
    return 1.0 if level == 0 else 2.0 ** (-(level - 1) / 2.0)


def dot(a, b):
    return jnp.dot(a, b, preferred_element_type=F32)


def dot_nt(a, b):
    return lax.dot_general(a, b, (((1,), (1,)), ((), ())), preferred_element_type=F32)


def kernel(
    q_hbm, k_hbm, v_hbm, g_hbm, lc_hbm, st_hbm,
    qo_ref, k_ref, v_ref, k_acc, v_acc, gs_ref, co_ref,
    q_ref, g_ref, lc_ref, st_ref, load_sem,
    q_t, k_t, g_t, masks, s_loc, g_loc, w_st, gw_st,
    grads, core_in, pair_sum, l0_in, l1_in, l2_in, y_in, y_sum,
    z5_in, z4_in, z3_in, state, near, coef_all,
    relay_sem, core_ss, core_rs, l0_ss, l0_rs, l1_ss, l1_rs, l2_ss, l2_rs, y_ss, y_rs,
    z5_ss, z5_rs, z4_ss, z4_rs, z3_ss, z3_rs, st_ss, st_rs, nr_ss, nr_rs, x_ss, x_rs,
):
    shard = lax.axis_index("seq")
    hx = lax.axis_index("head")
    c = lax.rem(shard, 2)
    y = lax.rem(shard // 2, 4)
    z = shard // 8

    def at(cc, yy, zz):
        return ((zz * 4 + yy) * 2 + cc, hx)

    def bit(j):
        return lax.rem(shard // (1 << j), 2)

    other = 1 - c
    plane = [(cc, k) for cc in range(2) for k in range(4) if cc or k]

    def plane_dev(cc, k):
        return lax.rem(c + cc, 2), lax.rem(y + k, 4)

    order = [pl.ds(pl.multiple_of(n * BLK, BLK), BLK) for n in (other, c)]
    pairs = []
    for hs in order:
        pairs += [(g_hbm.at[:, hs], g_ref.at[:, hs]), (q_hbm.at[:, hs], q_ref.at[:, hs])]
    pairs.insert(1, (lc_hbm, lc_ref))
    pairs += [(k_hbm, k_ref), (v_hbm, v_ref), (st_hbm, st_ref)]
    loads = [pltpu.make_async_copy(src, dst, load_sem.at[n]) for n, (src, dst) in enumerate(pairs)]
    for load in loads:
        load.start()

    barrier = pltpu.get_barrier_semaphore()
    for cc, k in plane:
        pc, py = plane_dev(cc, k)
        pl.semaphore_signal(barrier, inc=1, device_id=at(pc, py, z), device_id_type=MESH)
    for k in (1, 7):
        pl.semaphore_signal(barrier, inc=1, device_id=at(c, y, lax.rem(z + k, 8)), device_id_type=MESH)
    for k in range(1, 4):
        pl.semaphore_signal(barrier, inc=1, device_id=(shard, lax.rem(hx + k, 4)), device_id_type=MESH)

    bits = [bit(j).astype(F32) for j in range(CROSS)]

    def block(i, carry):
        ts = pl.ds(pl.multiple_of(i * BLK, BLK), BLK)
        slots = (i // 2, 4 + i // 4, 6)
        right = [lax.rem(i // (1 << n), 2).astype(F32) for n in range(3)]
        rows = [lc_ref[n : n + 1, ts] for n in range(DIAG)]
        coef = masks[0] * rows[0]
        for n in range(1, DIAG):
            coef = coef + masks[n] * rows[n]
        local = [lc_ref[DIAG + n : DIAG + n + 1, ts] * (right[n] * level_weight(DIAG + n)) for n in range(3)]
        cross = [lc_ref[LOCAL + j : LOCAL + j + 1, ts] * bits[j] for j in range(CROSS)]
        prods = None
        sums = [None] * (3 + CROSS)
        for h in range(2):
            hs = slice(h * BLK, (h + 1) * BLK)
            k_i, v_i = k_ref[ts, hs], v_ref[ts, hs]
            qt, kt, gt = q_t[h, :, ts], k_t[h, :, ts], g_t[h, :, ts]
            scores = dot(k_i, qt)
            grad_scores = dot(v_i, gt)
            prod = scores * grad_scores
            prods = prod if prods is None else prods + prod
            weights = (coef * scores).astype(BF16)
            grad_weights = (coef * grad_scores).astype(BF16)
            w_st[h, i] = weights
            gw_st[h, i] = grad_weights
            acc = dot(kt, grad_weights)
            qf = qt.astype(F32)
            for n in range(3 + CROSS):
                s = s_loc[h, slots[n]] if n < 3 else st_ref[0, n - 3, h]
                projected = dot(s, gt)
                acc = acc + projected * (local[n] if n < 3 else cross[n - 3])
                part = jnp.sum(qf * projected, axis=0, keepdims=True)
                sums[n] = part if sums[n] is None else sums[n] + part
            qo_ref[ts, hs] = acc.T.astype(BF16)
        for n in range(DIAG):
            coef_all[hx, n : n + 1, ts] = jnp.sum(masks[n] * prods, axis=0, keepdims=True)
        for n in range(3):
            coef_all[hx, DIAG + n : DIAG + n + 1, ts] = sums[n] * (right[n] * level_weight(DIAG + n))
        for j in range(CROSS):
            coef_all[hx, LOCAL + j : LOCAL + j + 1, ts] = sums[3 + j] * bits[j]
        return carry

    sends = []

    def copy(src, dst, ss, rs, dev):
        return pltpu.make_async_remote_copy(
            src_ref=src, dst_ref=dst, send_sem=ss, recv_sem=rs, device_id=dev, device_id_type=MESH
        )

    def send(cond, *args):
        def go():
            copy(*args).start()

        def done():
            copy(*args).wait_send()

        if cond is None:
            go()
        else:
            pl.when(cond)(go)
        sends.append((cond, done))

    mate = at(other, y, z)

    def state_grad(j, n, hs):
        row = lc_ref[LOCAL + j : LOCAL + j + 1, :]
        scaled = (g_t[n].astype(F32) * row).astype(BF16)
        grads[j, n] = (level_weight(LOCAL + j) * dot(scaled, q_ref[:, hs])).reshape(4, 32, BLK)

    def core_send(j):
        send(bit(j) == 1, grads.at[j, other], core_in.at[j], core_ss.at[j], core_rs.at[j], mate)

    loads[0].wait()
    g_t[other] = g_ref[:, order[0]].T
    loads[1].wait()
    loads[2].wait()
    for j in (5, 4, 3, 2, 1):
        state_grad(j, other, order[0])
    pl.semaphore_wait(barrier, len(plane) + 2 + 3)

    def relay(step):
        far = 1 << step
        for way, k in enumerate((far, 8 - far)):
            pl.semaphore_signal(
                relay_sem.at[step, way], inc=1, device_id=at(c, y, lax.rem(z + k, 8)), device_id_type=MESH
            )

    def relayed(step):
        for way in range(2):
            pl.semaphore_wait(relay_sem.at[step, way], 1)

    for j in (5, 4, 3, 2, 1):
        core_send(j)
    relay(0)
    loads[3].wait()
    g_t[c] = g_ref[:, order[1]].T
    loads[4].wait()
    for j in reversed(range(CROSS)):
        state_grad(j, c, order[1])
    state_grad(0, other, order[0])
    relayed(0)
    relay(1)

    def y_send(n, k):
        py = lax.rem(y + k, 4)
        src = z3_in.at[py] if n == 0 else pair_sum.at[FAR[n], py]
        return (src, y_in.at[n, k - 1], y_ss.at[n, k - 1], y_rs.at[n, k - 1], at(c, py, z))

    for j in (5, 4, 3, 2, 1):
        on = bit(j) == 1

        @pl.when(on)
        def _():
            copy(grads.at[j, other], core_in.at[j], core_ss.at[j], core_rs.at[j], mate).wait_recv()
            pair_sum[j] = grads[j, c] + core_in[j]

        if j >= 4:
            for k in range(1, 4):
                send(on, *y_send(FAR.index(j), k))
        elif j == 3:
            send(on, pair_sum.at[3], z3_in, z3_ss, z3_rs, at(c, y, z - 1))

    send(c == 1, grads.at[0], l0_in, l0_ss, l0_rs, mate)

    key_pos = lax.broadcasted_iota(jnp.int32, (BLK, BLK), 0)
    query_pos = lax.broadcasted_iota(jnp.int32, (BLK, BLK), 1)
    mixed = jnp.bitwise_xor(key_pos, query_pos)
    level = jnp.zeros((BLK, BLK), jnp.int32)
    for b in range(DIAG - 1):
        level = level + (mixed >= (1 << b)).astype(jnp.int32)
    for n in range(DIAG):
        hit = jnp.logical_and(level == n, key_pos <= query_pos)
        masks[n] = jnp.where(hit, level_weight(n), 0.0).astype(F32)

    for n in range(5, 8):
        loads[n].wait()
    for h in range(2):
        hs = slice(h * BLK, (h + 1) * BLK)
        q_t[h] = q_ref[:, hs].T
        k_t[h] = k_ref[:, hs].T

    for h in range(2):
        hs = slice(h * BLK, (h + 1) * BLK)
        for n in range(4):
            r = slice(n * 256, n * 256 + 128)
            s_loc[h, n] = dot(k_t[h, :, r], v_ref[r, hs]).astype(BF16)
        for n in range(2):
            r = slice(n * 512, n * 512 + 256)
            s_loc[h, 4 + n] = dot(k_t[h, :, r], v_ref[r, hs]).astype(BF16)
        s_loc[h, 6] = dot(k_t[h, :, 0:512], v_ref[0:512, hs]).astype(BF16)

    lax.fori_loop(0, 2, block, 0, unroll=2)

    relayed(1)
    z5 = lambda k: (y_sum.at[2], z5_in.at[z - 4], z5_ss.at[k], z5_rs.at[z - 4], at(c, y, k))
    z4 = lambda k: (
        y_sum.at[1], z4_in.at[lax.rem(z, 2)], z4_ss.at[k], z4_rs.at[lax.rem(z, 2)], at(c, y, (z // 4) * 4 + k)
    )
    for n in (2, 1):
        on = bit(FAR[n]) == 1

        @pl.when(on)
        def _():
            total = pair_sum[FAR[n], y]
            for k in range(1, 4):
                copy(*y_send(n, k)).wait_recv()
                total = total + y_in[n, k - 1]
            y_sum[n] = total

        for k in range(4 if n == 2 else 2):
            send(on, *(z5(k) if n == 2 else z4(k)))

    even = bit(3) == 0

    @pl.when(even)
    def _():
        copy(pair_sum.at[3], z3_in, z3_ss, z3_rs, at(c, y, z)).wait_recv()

    for k in range(1, 4):
        send(even, *y_send(0, k))

    for k in range(2):
        send(bit(2) == 1, pair_sum.at[2], l2_in.at[y - 2], l2_ss.at[k], l2_rs.at[y - 2], at(c, k, z))
    send(bit(1) == 1, pair_sum.at[1], l1_in, l1_ss, l1_rs, at(c, y - 1, z))

    lax.fori_loop(2, NB, block, 0, unroll=2)

    for k in range(1, 4):
        send(
            None, coef_all.at[hx], coef_all.at[hx], x_ss.at[k - 1], x_rs.at[k - 1],
            (shard, lax.rem(hx + k, 4)),
        )

    near[c] = jnp.zeros((4, 32, BLK), F32)

    @pl.when(bit(2) == 0)
    def _():
        for k in range(2):
            copy(pair_sum.at[2], l2_in.at[k], l2_ss.at[k], l2_rs.at[k], at(c, y, z)).wait_recv()
        near[c] += l2_in[0] + l2_in[1]

    @pl.when(bit(1) == 0)
    def _():
        copy(pair_sum.at[1], l1_in, l1_ss, l1_rs, at(c, y, z)).wait_recv()
        near[c] += l1_in[...]

    send(None, near.at[c], near.at[c], nr_ss, nr_rs, mate)

    some = z < 7

    @pl.when(z == 7)
    def _():
        state[...] = jnp.zeros_like(state)

    @pl.when(some)
    def _():
        state[c, y] = jnp.zeros((32, BLK), F32)

    @pl.when(even)
    def _():
        total = z3_in[y]
        for k in range(1, 4):
            copy(*y_send(0, k)).wait_recv()
            total = total + y_in[0, k - 1]
        state[c, y] += total

    @pl.when(bit(4) == 0)
    def _():
        for k in range(2):
            copy(y_sum.at[1], z4_in.at[k], z4_ss.at[k], z4_rs.at[k], at(c, y, z)).wait_recv()
        state[c, y] += z4_in[0] + z4_in[1]

    @pl.when(bit(5) == 0)
    def _():
        for k in range(4):
            copy(y_sum.at[2], z5_in.at[k], z5_ss.at[k], z5_rs.at[k], at(c, y, z)).wait_recv()
        state[c, y] += (z5_in[0] + z5_in[1]) + (z5_in[2] + z5_in[3])

    for n, (cc, k) in enumerate(plane):
        pc, py = plane_dev(cc, k)
        send(some, state.at[c, y], state.at[c, y], st_ss.at[n], st_rs.at[n], at(pc, py, z))

    for h in range(2):
        hs = slice(h * BLK, (h + 1) * BLK)
        for n in range(7):
            lev = 0 if n < 4 else 1 if n < 6 else 2
            half = BLK << lev
            start = (2 * (n - (0, 4, 6)[lev]) + 1) * half
            r = slice(start, start + half)
            row = lc_ref[DIAG + lev : DIAG + lev + 1, r] * level_weight(DIAG + lev)
            g_loc[h, n] = dot((g_t[h, :, r].astype(F32) * row).astype(BF16), q_ref[r, hs])
        for i in range(NB):
            ts = slice(i * BLK, (i + 1) * BLK)
            k_acc[ts, hs] = dot(gw_st[h, i], q_ref[ts, hs])
            v_acc[ts, hs] = dot(w_st[h, i], g_ref[ts, hs])

    for k in range(1, 4):
        px = lax.rem(hx + 4 - k, 4)
        copy(
            coef_all.at[px], coef_all.at[px], x_ss.at[k - 1], x_rs.at[k - 1], (shard, px)
        ).wait_recv()
    co_ref[...] = ((coef_all[0] + coef_all[1]) + (coef_all[2] + coef_all[3]))

    copy(near.at[other], near.at[other], nr_ss, nr_rs, mate).wait_recv()

    @pl.when(c == 0)
    def _():
        copy(grads.at[0], l0_in, l0_ss, l0_rs, mate).wait_recv()

    @pl.when(c == 1)
    def _():
        l0_in[...] = jnp.zeros_like(l0_in)

    @pl.when(some)
    def _():
        for n, (cc, k) in enumerate(plane):
            sc, sy = lax.rem(c + cc, 2), lax.rem(y + 4 - k, 4)
            copy(state.at[sc, sy], state.at[sc, sy], st_ss.at[n], st_rs.at[n], at(sc, sy, z)).wait_recv()

    for h in range(2):
        base = (state[h] + (near[h] + l0_in[h])).reshape(BLK, BLK)
        for i in range(NB):
            total = base
            for n, slot in enumerate((i // 2, 4 + i // 4, 6)):
                if (i >> n) % 2 == 0:
                    total = total + g_loc[h, slot]
            gs_ref[h, i] = total.astype(BF16)

    for cond, done in sends:
        if cond is None:
            done()
        else:
            pl.when(cond)(done)


def finish(
    qi_ref, k_ref, v_ref, k_acc, v_acc, gs_ref, ci_ref,
    qo_hbm, ko_hbm, vo_hbm, co_hbm,
    ko, vo, sem,
):
    writes = [
        pltpu.make_async_copy(qi_ref, qo_hbm, sem.at[0]),
        pltpu.make_async_copy(ci_ref, co_hbm, sem.at[1]),
    ]
    for write in writes:
        write.start()
    for i in range(NB):
        ts = slice(i * BLK, (i + 1) * BLK)
        for h in range(2):
            hs = slice(h * BLK, (h + 1) * BLK)
            gs = gs_ref[h, i]
            ko[ts, hs] = (k_acc[ts, hs] + dot(v_ref[ts, hs], gs)).astype(BF16)
            vo[ts, hs] = (v_acc[ts, hs] + dot_nt(k_ref[ts, hs], gs)).astype(BF16)
        for n, (src, dst) in enumerate(((ko, ko_hbm), (vo, vo_hbm))):
            write = pltpu.make_async_copy(src.at[ts], dst.at[ts], sem.at[2 + 2 * i + n])
            write.start()
            writes.append(write)
    for write in writes:
        write.wait()


def shards(queries, key_vectors, values, out_grad, level_coef, saved_states):
    sem = pltpu.SemaphoreType.DMA
    quarter = (4, 32, BLK)
    vmem = pl.BlockSpec(memory_space=pltpu.VMEM)
    hbm = pl.BlockSpec(memory_space=pltpu.HBM)
    tokens = jax.ShapeDtypeStruct((TOK, 2 * BLK), BF16)
    sums = jax.ShapeDtypeStruct((TOK, 2 * BLK), F32)
    coefs = jax.ShapeDtypeStruct((LOCAL + CROSS, TOK), F32)
    parts = pl.pallas_call(
            kernel,
            out_shape=[tokens] * 3 + [sums] * 2 + [jax.ShapeDtypeStruct((2, NB, BLK, BLK), BF16), coefs],
            in_specs=[hbm] * 6,
            out_specs=[vmem] * 7,
            scratch_shapes=[
                pltpu.VMEM((TOK, 2 * BLK), BF16),
                pltpu.VMEM((TOK, 2 * BLK), BF16),
                pltpu.VMEM((LOCAL + CROSS, TOK), F32),
                pltpu.VMEM((1, CROSS, 2, BLK, BLK), BF16),
                sem((8,)),
                pltpu.VMEM((2, BLK, TOK), BF16),
                pltpu.VMEM((2, BLK, TOK), BF16),
                pltpu.VMEM((2, BLK, TOK), BF16),
                pltpu.VMEM((DIAG, BLK, BLK), F32),
                pltpu.VMEM((2, 7, BLK, BLK), BF16),
                pltpu.VMEM((2, 7, BLK, BLK), F32),
                pltpu.VMEM((2, NB, BLK, BLK), BF16),
                pltpu.VMEM((2, NB, BLK, BLK), BF16),
                pltpu.VMEM((CROSS, 2) + quarter, F32),
                pltpu.VMEM((CROSS,) + quarter, F32),
                pltpu.VMEM((CROSS,) + quarter, F32),
                pltpu.VMEM((2,) + quarter, F32),
                pltpu.VMEM(quarter, F32),
                pltpu.VMEM((2,) + quarter, F32),
                pltpu.VMEM((3, 3, 32, BLK), F32),
                pltpu.VMEM((3, 32, BLK), F32),
                pltpu.VMEM((4, 32, BLK), F32),
                pltpu.VMEM((2, 32, BLK), F32),
                pltpu.VMEM(quarter, F32),
                pltpu.VMEM((2,) + quarter, F32),
                pltpu.VMEM((2,) + quarter, F32),
                pltpu.VMEM((4, LOCAL + CROSS, TOK), F32),
                pltpu.SemaphoreType.REGULAR((2, 2)),
                sem((CROSS,)), sem((CROSS,)),
                sem, sem,
                sem, sem,
                sem((2,)), sem((2,)),
                sem((3, 3)), sem((3, 3)),
                sem((4,)), sem((4,)),
                sem((2,)), sem((2,)),
                sem, sem,
                sem((7,)), sem((7,)),
                sem, sem,
                sem((3,)), sem((3,)),
            ],
            compiler_params=pltpu.CompilerParams(
                collective_id=0, has_side_effects=True, vmem_limit_bytes=40 * 2**20
            ),
        )(*[pltpu.with_memory_space_constraint(a, pltpu.HBM) for a in (queries, key_vectors, values, out_grad, level_coef, saved_states)])
    return tuple(
        pl.pallas_call(
            finish,
            out_shape=[tokens] * 3 + [coefs],
            in_specs=[vmem] * 7,
            out_specs=[hbm] * 4,
            scratch_shapes=[
                pltpu.VMEM((TOK, 2 * BLK), BF16),
                pltpu.VMEM((TOK, 2 * BLK), BF16),
                sem((2 + 2 * NB,)),
            ],
            compiler_params=pltpu.CompilerParams(vmem_limit_bytes=16 * 2**20),
        )(*parts)
    )


def solution(mesh):
    in_specs = (
        P("seq", "head"),
        P("seq", "head"),
        P("seq", "head"),
        P("seq", "head"),
        P(None, "seq"),
        P("seq", None, "head", None, None),
    )
    out_specs = (P("seq", "head"), P("seq", "head"), P("seq", "head"), P(None, "seq"))
    return jax.shard_map(shards, mesh=mesh, in_specs=in_specs, out_specs=out_specs, check_vma=False)
```

```python
import jax
import jax.numpy as jnp
from jax import lax
from jax.experimental import pallas as pl
from jax.experimental.pallas import tpu as pltpu
from jax.sharding import PartitionSpec as P

MESH = pl.DeviceIdType.MESH
F32 = jnp.float32
BF16 = jnp.bfloat16
TOK = 1024
BLK = 128
NB = TOK // BLK
LOCAL = 11
CROSS = 6
DIAG = 8
FAR = (3, 4, 5)


def level_weight(level):
    return 1.0 if level == 0 else 2.0 ** (-(level - 1) / 2.0)


def dot(a, b):
    return jnp.dot(a, b, preferred_element_type=F32)


def dot_nt(a, b):
    return lax.dot_general(a, b, (((1,), (1,)), ((), ())), preferred_element_type=F32)


def kernel(
    q_hbm, k_hbm, v_hbm, g_hbm, lc_hbm, st_hbm,
    qo_ref, k_ref, v_ref, k_acc, v_acc, gs_ref, co_ref,
    q_ref, g_ref, lc_ref, st_ref, load_sem,
    q_t, k_t, g_t, masks, s_loc, g_loc, w_st, gw_st,
    grads, core_in, pair_sum, l0_in, l1_in, l2_in, y_in, y_sum,
    z5_in, z4_in, z3_in, state, near, coef_all,
    relay_sem, core_ss, core_rs, l0_ss, l0_rs, l1_ss, l1_rs, l2_ss, l2_rs, y_ss, y_rs,
    z5_ss, z5_rs, z4_ss, z4_rs, z3_ss, z3_rs, st_ss, st_rs, nr_ss, nr_rs, x_ss, x_rs,
):
    shard = lax.axis_index("seq")
    hx = lax.axis_index("head")
    c = lax.rem(shard, 2)
    y = lax.rem(shard // 2, 4)
    z = shard // 8

    def at(cc, yy, zz):
        return ((zz * 4 + yy) * 2 + cc, hx)

    def bit(j):
        return lax.rem(shard // (1 << j), 2)

    other = 1 - c
    plane = [(cc, k) for cc in range(2) for k in range(4) if cc or k]

    def plane_dev(cc, k):
        return lax.rem(c + cc, 2), lax.rem(y + k, 4)

    order = [pl.ds(pl.multiple_of(n * BLK, BLK), BLK) for n in (other, c)]
    pairs = []
    for hs in order:
        pairs += [(g_hbm.at[:, hs], g_ref.at[:, hs]), (q_hbm.at[:, hs], q_ref.at[:, hs])]
    pairs.insert(1, (lc_hbm, lc_ref))
    pairs += [(k_hbm, k_ref), (v_hbm, v_ref), (st_hbm, st_ref)]
    loads = [
        pltpu.make_async_copy(src, dst, load_sem.at[(0, 1, 2, 3, 3, 4, 5, 6)[n]]) for n, (src, dst) in enumerate(pairs)
    ]
    for load in loads:
        load.start()

    barrier = pltpu.get_barrier_semaphore()
    for cc, k in plane:
        pc, py = plane_dev(cc, k)
        pl.semaphore_signal(barrier, inc=1, device_id=at(pc, py, z), device_id_type=MESH)
    for k in (1, 7):
        pl.semaphore_signal(barrier, inc=1, device_id=at(c, y, lax.rem(z + k, 8)), device_id_type=MESH)
    for k in range(1, 4):
        pl.semaphore_signal(barrier, inc=1, device_id=(shard, lax.rem(hx + k, 4)), device_id_type=MESH)

    bits = [bit(j).astype(F32) for j in range(CROSS)]

    def block(i, carry):
        ts = pl.ds(pl.multiple_of(i * BLK, BLK), BLK)
        slots = (i // 2, 4 + i // 4, 6)
        right = [lax.rem(i // (1 << n), 2).astype(F32) for n in range(3)]
        rows = [lc_ref[n : n + 1, ts] for n in range(DIAG)]
        coef = masks[0] * rows[0]
        for n in range(1, DIAG):
            coef = coef + masks[n] * rows[n]
        local = [lc_ref[DIAG + n : DIAG + n + 1, ts] * (right[n] * level_weight(DIAG + n)) for n in range(3)]
        cross = [lc_ref[LOCAL + j : LOCAL + j + 1, ts] * bits[j] for j in range(CROSS)]
        prods = None
        sums = [None] * (3 + CROSS)
        for h in range(2):
            hs = slice(h * BLK, (h + 1) * BLK)
            k_i, v_i = k_ref[ts, hs], v_ref[ts, hs]
            qt, kt, gt = q_t[h, :, ts], k_t[h, :, ts], g_t[h, :, ts]
            scores = dot(k_i, qt)
            grad_scores = dot(v_i, gt)
            prod = scores * grad_scores
            prods = prod if prods is None else prods + prod
            weights = (coef * scores).astype(BF16)
            grad_weights = (coef * grad_scores).astype(BF16)
            w_st[h, i] = weights
            gw_st[h, i] = grad_weights
            acc = dot(kt, grad_weights)
            qf = qt.astype(F32)
            for n in range(3 + CROSS):
                s = s_loc[h, slots[n]] if n < 3 else st_ref[0, n - 3, h]
                projected = dot(s, gt)
                acc = acc + projected * (local[n] if n < 3 else cross[n - 3])
                part = jnp.sum(qf * projected, axis=0, keepdims=True)
                sums[n] = part if sums[n] is None else sums[n] + part
            qo_ref[ts, hs] = acc.T.astype(BF16)
        for n in range(DIAG):
            coef_all[hx, n : n + 1, ts] = jnp.sum(masks[n] * prods, axis=0, keepdims=True)
        for n in range(3):
            coef_all[hx, DIAG + n : DIAG + n + 1, ts] = sums[n] * (right[n] * level_weight(DIAG + n))
        for j in range(CROSS):
            coef_all[hx, LOCAL + j : LOCAL + j + 1, ts] = sums[3 + j] * bits[j]
        return carry

    sends = []

    def copy(src, dst, ss, rs, dev):
        return pltpu.make_async_remote_copy(
            src_ref=src, dst_ref=dst, send_sem=ss, recv_sem=rs, device_id=dev, device_id_type=MESH
        )

    def send(cond, *args):
        def go():
            copy(*args).start()

        if cond is None:
            go()
        else:
            pl.when(cond)(go)

    def sent(cond, ref, ss):
        sends.append((cond, lambda: copy(ref, ref, ss, ss, mate).wait_send()))

    def received(ref, rs):
        copy(ref, ref, rs, rs, mate).wait_recv()

    mate = at(other, y, z)

    def state_grad(j, n, hs):
        row = lc_ref[LOCAL + j : LOCAL + j + 1, :]
        scaled = (g_t[n].astype(F32) * row).astype(BF16)
        grads[j, n] = (level_weight(LOCAL + j) * dot(scaled, q_ref[:, hs])).reshape(4, 32, BLK)

    def core_send(j):
        group = (2, 2, 2, 2, 1, 0)[j]
        send(None, grads.at[j, other], core_in.at[j], core_ss, core_rs.at[group], mate)

    loads[0].wait()
    g_t[other] = g_ref[:, order[0]].T
    loads[1].wait()
    loads[2].wait()
    for j in (5, 4, 3, 2, 1):
        state_grad(j, other, order[0])
    pl.semaphore_wait(barrier, len(plane) + 2 + 3)

    def relay(step):
        far = 1 << step
        for k in (far, 8 - far):
            pl.semaphore_signal(
                relay_sem.at[step], inc=1, device_id=at(c, y, lax.rem(z + k, 8)), device_id_type=MESH
            )

    def relayed(step):
        pl.semaphore_wait(relay_sem.at[step], 2)

    for j in (5, 4, 3, 2, 1):
        core_send(j)
    sent(None, core_in.at[pl.ds(1, 5)], core_ss)
    relay(0)
    pltpu.make_async_copy(g_ref, g_ref, load_sem.at[3]).wait()
    g_t[c] = g_ref[:, order[1]].T
    for j in reversed(range(CROSS)):
        state_grad(j, c, order[1])
    state_grad(0, other, order[0])
    relayed(0)
    relay(1)

    def y_send(n, k):
        py = lax.rem(y + k, 4)
        src = z3_in.at[py] if n == 0 else pair_sum.at[FAR[n], py]
        return (src, y_in.at[n, k - 1], y_ss.at[n], y_rs.at[n], at(c, py, z))

    for j in (5, 4, 3, 2, 1):
        on = bit(j) == 1

        if j >= 4:
            received(core_in.at[j], core_rs.at[5 - j])
        elif j == 3:
            received(core_in.at[pl.ds(1, 3)], core_rs.at[2])
        pair_sum[j] = grads[j, c] + core_in[j]
        if j >= 4:
            n = FAR.index(j)

            @pl.when(on)
            def _():
                for k in range(1, 4):
                    copy(*y_send(n, k)).start()

            sent(on, y_in.at[n], y_ss.at[n])
        elif j == 3:
            send(on, pair_sum.at[3], z3_in, z3_ss, z3_rs, at(c, y, z - 1))
            sent(on, z3_in, z3_ss)

    send(c == 1, grads.at[0], l0_in, l0_ss, l0_rs, mate)
    sent(c == 1, l0_in, l0_ss)

    key_pos = lax.broadcasted_iota(jnp.int32, (BLK, BLK), 0)
    query_pos = lax.broadcasted_iota(jnp.int32, (BLK, BLK), 1)
    mixed = jnp.bitwise_xor(key_pos, query_pos)
    level = jnp.zeros((BLK, BLK), jnp.int32)
    for b in range(DIAG - 1):
        level = level + (mixed >= (1 << b)).astype(jnp.int32)
    for n in range(DIAG):
        hit = jnp.logical_and(level == n, key_pos <= query_pos)
        masks[n] = jnp.where(hit, level_weight(n), 0.0).astype(F32)

    for n in range(5, 8):
        loads[n].wait()
    for h in range(2):
        hs = slice(h * BLK, (h + 1) * BLK)
        q_t[h] = q_ref[:, hs].T
        k_t[h] = k_ref[:, hs].T

    for h in range(2):
        hs = slice(h * BLK, (h + 1) * BLK)
        for n in range(4):
            r = slice(n * 256, n * 256 + 128)
            s_loc[h, n] = dot(k_t[h, :, r], v_ref[r, hs]).astype(BF16)
        for n in range(2):
            r = slice(n * 512, n * 512 + 256)
            s_loc[h, 4 + n] = dot(k_t[h, :, r], v_ref[r, hs]).astype(BF16)
        s_loc[h, 6] = dot(k_t[h, :, 0:512], v_ref[0:512, hs]).astype(BF16)

    lax.fori_loop(0, 2, block, 0, unroll=2)

    relayed(1)
    def z5(k):
        return (y_sum.at[2], z5_in.at[z - 4], z5_ss, z5_rs, at(c, y, lax.rem(z + k, 4)))

    def z4(k):
        slot = lax.rem(z, 2)
        return (y_sum.at[1], z4_in.at[slot], z4_ss, z4_rs, at(c, y, (z // 4) * 4 + lax.rem(slot + k, 2)))

    for n, dests, z_send, z_in, ss in ((2, (0, 1, 3, 2), z5, z5_in, z5_ss), (1, (0, 1), z4, z4_in, z4_ss)):
        on = bit(FAR[n]) == 1

        @pl.when(on)
        def _():
            received(y_in.at[n], y_rs.at[n])
            y_sum[n] = pair_sum[FAR[n], y] + (y_in[n, 0] + (y_in[n, 1] + y_in[n, 2]))
            for k in dests:
                copy(*z_send(k)).start()

        sent(on, z_in, ss)

    even = bit(3) == 0

    @pl.when(even)
    def _():
        received(z3_in, z3_rs)
        for k in range(1, 4):
            copy(*y_send(0, k)).start()

    sent(even, y_in.at[0], y_ss.at[0])

    for k in range(2):
        send(bit(2) == 1, pair_sum.at[2], l2_in.at[y - 2], l2_ss, l2_rs, at(c, k, z))
    sent(bit(2) == 1, l2_in, l2_ss)
    send(bit(1) == 1, pair_sum.at[1], l1_in, l1_ss, l1_rs, at(c, y - 1, z))
    sent(bit(1) == 1, l1_in, l1_ss)

    lax.fori_loop(2, NB, block, 0, unroll=2)

    for k in range(1, 4):
        send(
            None, coef_all.at[hx], coef_all.at[hx], x_ss, x_rs,
            (shard, lax.rem(hx + k, 4)),
        )
    sent(None, coef_all.at[pl.ds(0, 3)], x_ss)

    near[c] = jnp.zeros((4, 32, BLK), F32)

    @pl.when(bit(2) == 0)
    def _():
        received(l2_in, l2_rs)
        near[c] += l2_in[0] + l2_in[1]

    @pl.when(bit(1) == 0)
    def _():
        received(l1_in, l1_rs)
        near[c] += l1_in[...]

    send(None, near.at[c], near.at[c], nr_ss, nr_rs, mate)
    sent(None, near.at[c], nr_ss)

    some = z < 7

    @pl.when(z == 7)
    def _():
        state[...] = jnp.zeros_like(state)

    own = c * 4 + y

    @pl.when(some)
    def _():
        state[own] = jnp.zeros((32, BLK), F32)

    @pl.when(even)
    def _():
        received(y_in.at[0], y_rs.at[0])
        state[own] += z3_in[y] + (y_in[0, 0] + (y_in[0, 1] + y_in[0, 2]))

    @pl.when(bit(4) == 0)
    def _():
        received(z4_in, z4_rs)
        state[own] += z4_in[0] + z4_in[1]

    @pl.when(bit(5) == 0)
    def _():
        received(z5_in, z5_rs)
        state[own] += (z5_in[0] + z5_in[1]) + (z5_in[2] + z5_in[3])

    @pl.when(some)
    def _():
        for cc, k in plane:
            pc, py = plane_dev(cc, k)
            copy(state.at[own], state.at[own], st_ss, st_rs, at(pc, py, z)).start()

    sent(some, state.at[pl.ds(0, 7)], st_ss)

    for h in range(2):
        hs = slice(h * BLK, (h + 1) * BLK)
        for n in range(7):
            lev = 0 if n < 4 else 1 if n < 6 else 2
            half = BLK << lev
            start = (2 * (n - (0, 4, 6)[lev]) + 1) * half
            r = slice(start, start + half)
            row = lc_ref[DIAG + lev : DIAG + lev + 1, r] * level_weight(DIAG + lev)
            g_loc[h, n] = dot((g_t[h, :, r].astype(F32) * row).astype(BF16), q_ref[r, hs])
        for i in range(NB):
            ts = slice(i * BLK, (i + 1) * BLK)
            k_acc[ts, hs] = dot(gw_st[h, i], q_ref[ts, hs])
            v_acc[ts, hs] = dot(w_st[h, i], g_ref[ts, hs])

    received(coef_all.at[pl.ds(0, 3)], x_rs)
    co_ref[...] = ((coef_all[0] + coef_all[1]) + (coef_all[2] + coef_all[3]))

    received(near.at[other], nr_rs)

    @pl.when(c == 0)
    def _():
        received(l0_in, l0_rs)

    @pl.when(c == 1)
    def _():
        l0_in[...] = jnp.zeros_like(l0_in)

    @pl.when(some)
    def _():
        received(state.at[pl.ds(0, 7)], st_rs)

    for h in range(2):
        base = (state[4 * h : 4 * h + 4] + (near[h] + l0_in[h])).reshape(BLK, BLK)
        for i in range(NB):
            total = base
            for n, slot in enumerate((i // 2, 4 + i // 4, 6)):
                if (i >> n) % 2 == 0:
                    total = total + g_loc[h, slot]
            gs_ref[h, i] = total.astype(BF16)

    for cond, done in sends:
        if cond is None:
            done()
        else:
            pl.when(cond)(done)


def finish(
    qi_ref, k_ref, v_ref, k_acc, v_acc, gs_ref, ci_ref,
    qo_hbm, ko_hbm, vo_hbm, co_hbm,
    ko, vo, sem,
):
    writes = [
        pltpu.make_async_copy(qi_ref, qo_hbm, sem.at[0]),
        pltpu.make_async_copy(ci_ref, co_hbm, sem.at[1]),
    ]
    for write in writes:
        write.start()
    for i in range(NB):
        ts = slice(i * BLK, (i + 1) * BLK)
        for h in range(2):
            hs = slice(h * BLK, (h + 1) * BLK)
            gs = gs_ref[h, i]
            ko[ts, hs] = (k_acc[ts, hs] + dot(v_ref[ts, hs], gs)).astype(BF16)
            vo[ts, hs] = (v_acc[ts, hs] + dot_nt(k_ref[ts, hs], gs)).astype(BF16)
        for n, (src, dst) in enumerate(((ko, ko_hbm), (vo, vo_hbm))):
            write = pltpu.make_async_copy(src.at[ts], dst.at[ts], sem.at[2 + 2 * i + n])
            write.start()
            writes.append(write)
    for write in writes:
        write.wait()


def shards(queries, key_vectors, values, out_grad, level_coef, saved_states):
    sem = pltpu.SemaphoreType.DMA
    quarter = (4, 32, BLK)
    vmem = pl.BlockSpec(memory_space=pltpu.VMEM)
    hbm = pl.BlockSpec(memory_space=pltpu.HBM)
    tokens = jax.ShapeDtypeStruct((TOK, 2 * BLK), BF16)
    sums = jax.ShapeDtypeStruct((TOK, 2 * BLK), F32)
    coefs = jax.ShapeDtypeStruct((LOCAL + CROSS, TOK), F32)
    parts = pl.pallas_call(
            kernel,
            out_shape=[tokens] * 3 + [sums] * 2 + [jax.ShapeDtypeStruct((2, NB, BLK, BLK), BF16), coefs],
            in_specs=[hbm] * 6,
            out_specs=[vmem] * 7,
            scratch_shapes=[
                pltpu.VMEM((TOK, 2 * BLK), BF16),
                pltpu.VMEM((TOK, 2 * BLK), BF16),
                pltpu.VMEM((LOCAL + CROSS, TOK), F32),
                pltpu.VMEM((1, CROSS, 2, BLK, BLK), BF16),
                sem((7,)),
                pltpu.VMEM((2, BLK, TOK), BF16),
                pltpu.VMEM((2, BLK, TOK), BF16),
                pltpu.VMEM((2, BLK, TOK), BF16),
                pltpu.VMEM((DIAG, BLK, BLK), F32),
                pltpu.VMEM((2, 7, BLK, BLK), BF16),
                pltpu.VMEM((2, 7, BLK, BLK), F32),
                pltpu.VMEM((2, NB, BLK, BLK), BF16),
                pltpu.VMEM((2, NB, BLK, BLK), BF16),
                pltpu.VMEM((CROSS, 2) + quarter, F32),
                pltpu.VMEM((CROSS,) + quarter, F32),
                pltpu.VMEM((CROSS,) + quarter, F32),
                pltpu.VMEM((2,) + quarter, F32),
                pltpu.VMEM(quarter, F32),
                pltpu.VMEM((2,) + quarter, F32),
                pltpu.VMEM((3, 3, 32, BLK), F32),
                pltpu.VMEM((3, 32, BLK), F32),
                pltpu.VMEM((4, 32, BLK), F32),
                pltpu.VMEM((2, 32, BLK), F32),
                pltpu.VMEM(quarter, F32),
                pltpu.VMEM((8, 32, BLK), F32),
                pltpu.VMEM((2,) + quarter, F32),
                pltpu.VMEM((4, LOCAL + CROSS, TOK), F32),
                pltpu.SemaphoreType.REGULAR((2,)),
                sem, sem((3,)),
                sem, sem,
                sem, sem,
                sem, sem,
                sem((3,)), sem((3,)),
                sem, sem,
                sem, sem,
                sem, sem,
                sem, sem,
                sem, sem,
                sem, sem,
            ],
            compiler_params=pltpu.CompilerParams(
                collective_id=0, has_side_effects=True, vmem_limit_bytes=40 * 2**20
            ),
        )(*[pltpu.with_memory_space_constraint(a, pltpu.HBM) for a in (queries, key_vectors, values, out_grad, level_coef, saved_states)])
    return tuple(
        pl.pallas_call(
            finish,
            out_shape=[tokens] * 3 + [coefs],
            in_specs=[vmem] * 7,
            out_specs=[hbm] * 4,
            scratch_shapes=[
                pltpu.VMEM((TOK, 2 * BLK), BF16),
                pltpu.VMEM((TOK, 2 * BLK), BF16),
                sem((2 + 2 * NB,)),
            ],
            compiler_params=pltpu.CompilerParams(vmem_limit_bytes=16 * 2**20),
        )(*parts)
    )


def solution(mesh):
    in_specs = (
        P("seq", "head"),
        P("seq", "head"),
        P("seq", "head"),
        P("seq", "head"),
        P(None, "seq"),
        P("seq", None, "head", None, None),
    )
    out_specs = (P("seq", "head"), P("seq", "head"), P("seq", "head"), P(None, "seq"))
    return jax.shard_map(shards, mesh=mesh, in_specs=in_specs, out_specs=out_specs, check_vma=False)
```

```python
import jax
import jax.numpy as jnp
from jax import lax
from jax.experimental import pallas as pl
from jax.experimental.pallas import tpu as pltpu
from jax.sharding import PartitionSpec as P

MESH = pl.DeviceIdType.MESH
F32 = jnp.float32
BF16 = jnp.bfloat16
TOK = 1024
BLK = 128
NB = TOK // BLK
LOCAL = 11
CROSS = 6
DIAG = 8
FAR = (3, 4, 5)


def level_weight(level):
    return 1.0 if level == 0 else 2.0 ** (-(level - 1) / 2.0)


def dot(a, b):
    return jnp.dot(a, b, preferred_element_type=F32)


def dot_nt(a, b):
    return lax.dot_general(a, b, (((1,), (1,)), ((), ())), preferred_element_type=F32)


def kernel(
    q_hbm, k_hbm, v_hbm, g_hbm, lc_hbm, st_hbm,
    qo_ref, k_ref, v_ref, k_acc, v_acc, gs_ref, co_ref,
    q_ref, g_ref, lc_ref, st_ref, load_sem,
    q_t, k_t, g_t, masks, s_loc, g_loc, w_st, gw_st,
    grads, core_in, pair_sum, l0_in, l1_in, l2_in, p_in, y_in, y_sum,
    z5_in, z4_in, z3_in, state, near, coef_all,
    relay_sem, core_ss, core_rs, l0_ss, l0_rs, l1_ss, l1_rs, l2_ss, l2_rs, p_ss, p_rs, y_ss, y_rs,
    z5_ss, z5_rs, z4_ss, z4_rs, z3_ss, z3_rs, st_ss, st_rs, nr_ss, nr_rs, x_ss, x_rs,
):
    shard = lax.axis_index("seq")
    hx = lax.axis_index("head")
    c = lax.rem(shard, 2)
    y = lax.rem(shard // 2, 4)
    z = shard // 8

    def at(cc, yy, zz):
        return ((zz * 4 + yy) * 2 + cc, hx)

    def bit(j):
        return lax.rem(shard // (1 << j), 2)

    other = 1 - c
    plane = [(cc, k) for cc in range(2) for k in range(4) if cc or k]

    def plane_dev(cc, k):
        return lax.rem(c + cc, 2), lax.rem(y + k, 4)

    order = [pl.ds(pl.multiple_of(n * BLK, BLK), BLK) for n in (other, c)]
    pairs = []
    for hs in order:
        pairs += [(g_hbm.at[:, hs], g_ref.at[:, hs]), (q_hbm.at[:, hs], q_ref.at[:, hs])]
    pairs.insert(1, (lc_hbm, lc_ref))
    pairs += [(k_hbm, k_ref), (v_hbm, v_ref), (st_hbm, st_ref)]
    loads = [
        pltpu.make_async_copy(src, dst, load_sem.at[(0, 1, 2, 3, 3, 4, 5, 6)[n]]) for n, (src, dst) in enumerate(pairs)
    ]
    for load in loads:
        load.start()

    barrier = pltpu.get_barrier_semaphore()
    for cc, k in plane:
        pc, py = plane_dev(cc, k)
        pl.semaphore_signal(barrier, inc=1, device_id=at(pc, py, z), device_id_type=MESH)
    for k in (1, 7):
        pl.semaphore_signal(barrier, inc=1, device_id=at(c, y, lax.rem(z + k, 8)), device_id_type=MESH)
    for k in range(1, 4):
        pl.semaphore_signal(barrier, inc=1, device_id=(shard, lax.rem(hx + k, 4)), device_id_type=MESH)

    bits = [bit(j).astype(F32) for j in range(CROSS)]

    def block(i, carry):
        ts = pl.ds(pl.multiple_of(i * BLK, BLK), BLK)
        slots = (i // 2, 4 + i // 4, 6)
        right = [lax.rem(i // (1 << n), 2).astype(F32) for n in range(3)]
        rows = [lc_ref[n : n + 1, ts] for n in range(DIAG)]
        coef = masks[0] * rows[0]
        for n in range(1, DIAG):
            coef = coef + masks[n] * rows[n]
        local = [lc_ref[DIAG + n : DIAG + n + 1, ts] * (right[n] * level_weight(DIAG + n)) for n in range(3)]
        cross = [lc_ref[LOCAL + j : LOCAL + j + 1, ts] * bits[j] for j in range(CROSS)]
        prods = None
        sums = [None] * (3 + CROSS)
        for h in range(2):
            hs = slice(h * BLK, (h + 1) * BLK)
            k_i, v_i = k_ref[ts, hs], v_ref[ts, hs]
            qt, kt, gt = q_t[h, :, ts], k_t[h, :, ts], g_t[h, :, ts]
            scores = dot(k_i, qt)
            grad_scores = dot(v_i, gt)
            prod = scores * grad_scores
            prods = prod if prods is None else prods + prod
            weights = (coef * scores).astype(BF16)
            grad_weights = (coef * grad_scores).astype(BF16)
            w_st[h, i] = weights
            gw_st[h, i] = grad_weights
            acc = dot(kt, grad_weights)
            qf = qt.astype(F32)
            for n in range(3 + CROSS):
                s = s_loc[h, slots[n]] if n < 3 else st_ref[0, n - 3, h]
                projected = dot(s, gt)
                acc = acc + projected * (local[n] if n < 3 else cross[n - 3])
                part = jnp.sum(qf * projected, axis=0, keepdims=True)
                sums[n] = part if sums[n] is None else sums[n] + part
            qo_ref[ts, hs] = acc.T.astype(BF16)
        for n in range(DIAG):
            coef_all[hx, n : n + 1, ts] = jnp.sum(masks[n] * prods, axis=0, keepdims=True)
        for n in range(3):
            coef_all[hx, DIAG + n : DIAG + n + 1, ts] = sums[n] * (right[n] * level_weight(DIAG + n))
        for j in range(CROSS):
            coef_all[hx, LOCAL + j : LOCAL + j + 1, ts] = sums[3 + j] * bits[j]
        return carry

    sends = []

    def copy(src, dst, ss, rs, dev):
        return pltpu.make_async_remote_copy(
            src_ref=src, dst_ref=dst, send_sem=ss, recv_sem=rs, device_id=dev, device_id_type=MESH
        )

    def send(cond, *args):
        def go():
            copy(*args).start()

        if cond is None:
            go()
        else:
            pl.when(cond)(go)

    def sent(cond, ref, ss):
        sends.append((cond, lambda: copy(ref, ref, ss, ss, mate).wait_send()))

    def received(ref, rs):
        copy(ref, ref, rs, rs, mate).wait_recv()

    mate = at(other, y, z)

    def state_grad(j, n, hs):
        row = lc_ref[LOCAL + j : LOCAL + j + 1, :]
        scaled = (g_t[n].astype(F32) * row).astype(BF16)
        grads[j, n] = (level_weight(LOCAL + j) * dot(scaled, q_ref[:, hs])).reshape(4, 32, BLK)

    def core_send(j):
        send(None, grads.at[j, other], core_in.at[j], core_ss, core_rs, mate)

    loads[0].wait()
    g_t[other] = g_ref[:, order[0]].T
    loads[1].wait()
    loads[2].wait()
    pltpu.make_async_copy(g_ref, g_ref, load_sem.at[3]).wait()
    g_t[c] = g_ref[:, order[1]].T
    for j in (5, 4):
        for n in range(2):
            state_grad(j, (other, c)[n], order[n])
    pl.semaphore_wait(barrier, len(plane) + 2 + 3)

    def relay(step):
        far = 1 << step
        for k in (far, 8 - far):
            pl.semaphore_signal(
                relay_sem.at[step], inc=1, device_id=at(c, y, lax.rem(z + k, 8)), device_id_type=MESH
            )

    def relayed(step):
        pl.semaphore_wait(relay_sem.at[step], 2)

    for j in (5, 4):
        n = j - 4

        @pl.when(bit(j) == 1)
        def _():
            for m, (cc, k) in enumerate(plane):
                pc, py = plane_dev(cc, k)
                copy(grads.at[j, pc, py], p_in.at[n, m], p_ss.at[n], p_rs.at[n], at(pc, py, z)).start()

        sent(bit(j) == 1, p_in.at[n], p_ss.at[n])
    relay(0)
    for j in (3, 2, 1):
        for n in range(2):
            state_grad(j, (other, c)[n], order[n])
    for j in (3, 2, 1):
        core_send(j)
    sent(None, core_in.at[pl.ds(1, 3)], core_ss)
    state_grad(0, other, order[0])
    state_grad(0, c, order[1])
    relayed(0)
    relay(1)

    def y_send(n, k):
        py = lax.rem(y + k, 4)
        src = z3_in.at[py]
        return (src, y_in.at[n, k - 1], y_ss.at[n], y_rs.at[n], at(c, py, z))

    received(core_in.at[pl.ds(1, 3)], core_rs)
    for j in (3, 2, 1):
        pair_sum[j] = grads[j, c] + core_in[j]
    send(bit(3) == 1, pair_sum.at[3], z3_in, z3_ss, z3_rs, at(c, y, z - 1))
    sent(bit(3) == 1, z3_in, z3_ss)

    send(c == 1, grads.at[0], l0_in, l0_ss, l0_rs, mate)
    sent(c == 1, l0_in, l0_ss)

    key_pos = lax.broadcasted_iota(jnp.int32, (BLK, BLK), 0)
    query_pos = lax.broadcasted_iota(jnp.int32, (BLK, BLK), 1)
    mixed = jnp.bitwise_xor(key_pos, query_pos)
    level = jnp.zeros((BLK, BLK), jnp.int32)
    for b in range(DIAG - 1):
        level = level + (mixed >= (1 << b)).astype(jnp.int32)
    for n in range(DIAG):
        hit = jnp.logical_and(level == n, key_pos <= query_pos)
        masks[n] = jnp.where(hit, level_weight(n), 0.0).astype(F32)

    for n in range(5, 8):
        loads[n].wait()
    for h in range(2):
        hs = slice(h * BLK, (h + 1) * BLK)
        q_t[h] = q_ref[:, hs].T
        k_t[h] = k_ref[:, hs].T

    for h in range(2):
        hs = slice(h * BLK, (h + 1) * BLK)
        for n in range(4):
            r = slice(n * 256, n * 256 + 128)
            s_loc[h, n] = dot(k_t[h, :, r], v_ref[r, hs]).astype(BF16)
        for n in range(2):
            r = slice(n * 512, n * 512 + 256)
            s_loc[h, 4 + n] = dot(k_t[h, :, r], v_ref[r, hs]).astype(BF16)
        s_loc[h, 6] = dot(k_t[h, :, 0:512], v_ref[0:512, hs]).astype(BF16)

    lax.fori_loop(0, 2, block, 0, unroll=2)

    relayed(1)
    def z5(k):
        return (y_sum.at[2], z5_in.at[z - 4], z5_ss, z5_rs, at(c, y, lax.rem(z + k, 4)))

    def z4(k):
        slot = lax.rem(z, 2)
        return (y_sum.at[1], z4_in.at[slot], z4_ss, z4_rs, at(c, y, (z // 4) * 4 + lax.rem(slot + k, 2)))

    for n, dests, z_send, z_in, ss in ((2, (0, 1, 3, 2), z5, z5_in, z5_ss), (1, (0, 1), z4, z4_in, z4_ss)):
        on = bit(FAR[n]) == 1

        @pl.when(on)
        def _():
            received(p_in.at[n - 1], p_rs.at[n - 1])
            total = grads[FAR[n], c, y]
            for m in range(7):
                total = total + p_in[n - 1, m]
            y_sum[n] = total
            for k in dests:
                copy(*z_send(k)).start()

        sent(on, z_in, ss)

    even = bit(3) == 0

    @pl.when(even)
    def _():
        received(z3_in, z3_rs)
        for k in range(1, 4):
            copy(*y_send(0, k)).start()

    sent(even, y_in.at[0], y_ss.at[0])

    for k in range(2):
        send(bit(2) == 1, pair_sum.at[2], l2_in.at[y - 2], l2_ss, l2_rs, at(c, k, z))
    sent(bit(2) == 1, l2_in, l2_ss)
    send(bit(1) == 1, pair_sum.at[1], l1_in, l1_ss, l1_rs, at(c, y - 1, z))
    sent(bit(1) == 1, l1_in, l1_ss)

    lax.fori_loop(2, NB, block, 0, unroll=2)

    for k in range(1, 4):
        send(
            None, coef_all.at[hx], coef_all.at[hx], x_ss, x_rs,
            (shard, lax.rem(hx + k, 4)),
        )
    sent(None, coef_all.at[pl.ds(0, 3)], x_ss)

    near[c] = jnp.zeros((4, 32, BLK), F32)

    @pl.when(bit(2) == 0)
    def _():
        received(l2_in, l2_rs)
        near[c] += l2_in[0] + l2_in[1]

    @pl.when(bit(1) == 0)
    def _():
        received(l1_in, l1_rs)
        near[c] += l1_in[...]

    send(None, near.at[c], near.at[c], nr_ss, nr_rs, mate)
    sent(None, near.at[c], nr_ss)

    some = z < 7

    @pl.when(z == 7)
    def _():
        state[...] = jnp.zeros_like(state)

    own = c * 4 + y

    @pl.when(some)
    def _():
        state[own] = jnp.zeros((32, BLK), F32)

    @pl.when(even)
    def _():
        received(y_in.at[0], y_rs.at[0])
        state[own] += z3_in[y] + (y_in[0, 0] + (y_in[0, 1] + y_in[0, 2]))

    @pl.when(bit(4) == 0)
    def _():
        received(z4_in, z4_rs)
        state[own] += z4_in[0] + z4_in[1]

    @pl.when(bit(5) == 0)
    def _():
        received(z5_in, z5_rs)
        state[own] += (z5_in[0] + z5_in[1]) + (z5_in[2] + z5_in[3])

    @pl.when(some)
    def _():
        for cc, k in plane:
            pc, py = plane_dev(cc, k)
            copy(state.at[own], state.at[own], st_ss, st_rs, at(pc, py, z)).start()

    sent(some, state.at[pl.ds(0, 7)], st_ss)

    for h in range(2):
        hs = slice(h * BLK, (h + 1) * BLK)
        for n in range(7):
            lev = 0 if n < 4 else 1 if n < 6 else 2
            half = BLK << lev
            start = (2 * (n - (0, 4, 6)[lev]) + 1) * half
            r = slice(start, start + half)
            row = lc_ref[DIAG + lev : DIAG + lev + 1, r] * level_weight(DIAG + lev)
            g_loc[h, n] = dot((g_t[h, :, r].astype(F32) * row).astype(BF16), q_ref[r, hs])
        for i in range(NB):
            ts = slice(i * BLK, (i + 1) * BLK)
            k_acc[ts, hs] = dot(gw_st[h, i], q_ref[ts, hs])
            v_acc[ts, hs] = dot(w_st[h, i], g_ref[ts, hs])

    received(coef_all.at[pl.ds(0, 3)], x_rs)
    co_ref[...] = ((coef_all[0] + coef_all[1]) + (coef_all[2] + coef_all[3]))

    received(near.at[other], nr_rs)

    @pl.when(c == 0)
    def _():
        received(l0_in, l0_rs)

    @pl.when(c == 1)
    def _():
        l0_in[...] = jnp.zeros_like(l0_in)

    @pl.when(some)
    def _():
        received(state.at[pl.ds(0, 7)], st_rs)

    for h in range(2):
        base = (state[4 * h : 4 * h + 4] + (near[h] + l0_in[h])).reshape(BLK, BLK)
        for i in range(NB):
            total = base
            for n, slot in enumerate((i // 2, 4 + i // 4, 6)):
                if (i >> n) % 2 == 0:
                    total = total + g_loc[h, slot]
            gs_ref[h, i] = total.astype(BF16)

    for cond, done in sends:
        if cond is None:
            done()
        else:
            pl.when(cond)(done)


def finish(
    qi_ref, k_ref, v_ref, k_acc, v_acc, gs_ref, ci_ref,
    qo_hbm, ko_hbm, vo_hbm, co_hbm,
    ko, vo, sem,
):
    writes = [
        pltpu.make_async_copy(qi_ref, qo_hbm, sem.at[0]),
        pltpu.make_async_copy(ci_ref, co_hbm, sem.at[1]),
    ]
    for write in writes:
        write.start()
    for i in range(NB):
        ts = slice(i * BLK, (i + 1) * BLK)
        for h in range(2):
            hs = slice(h * BLK, (h + 1) * BLK)
            gs = gs_ref[h, i]
            ko[ts, hs] = (k_acc[ts, hs] + dot(v_ref[ts, hs], gs)).astype(BF16)
            vo[ts, hs] = (v_acc[ts, hs] + dot_nt(k_ref[ts, hs], gs)).astype(BF16)
        for n, (src, dst) in enumerate(((ko, ko_hbm), (vo, vo_hbm))):
            write = pltpu.make_async_copy(src.at[ts], dst.at[ts], sem.at[2 + 2 * i + n])
            write.start()
            writes.append(write)
    for write in writes:
        write.wait()


def shards(queries, key_vectors, values, out_grad, level_coef, saved_states):
    sem = pltpu.SemaphoreType.DMA
    quarter = (4, 32, BLK)
    vmem = pl.BlockSpec(memory_space=pltpu.VMEM)
    hbm = pl.BlockSpec(memory_space=pltpu.HBM)
    tokens = jax.ShapeDtypeStruct((TOK, 2 * BLK), BF16)
    sums = jax.ShapeDtypeStruct((TOK, 2 * BLK), F32)
    coefs = jax.ShapeDtypeStruct((LOCAL + CROSS, TOK), F32)
    parts = pl.pallas_call(
            kernel,
            out_shape=[tokens] * 3 + [sums] * 2 + [jax.ShapeDtypeStruct((2, NB, BLK, BLK), BF16), coefs],
            in_specs=[hbm] * 6,
            out_specs=[vmem] * 7,
            scratch_shapes=[
                pltpu.VMEM((TOK, 2 * BLK), BF16),
                pltpu.VMEM((TOK, 2 * BLK), BF16),
                pltpu.VMEM((LOCAL + CROSS, TOK), F32),
                pltpu.VMEM((1, CROSS, 2, BLK, BLK), BF16),
                sem((7,)),
                pltpu.VMEM((2, BLK, TOK), BF16),
                pltpu.VMEM((2, BLK, TOK), BF16),
                pltpu.VMEM((2, BLK, TOK), BF16),
                pltpu.VMEM((DIAG, BLK, BLK), F32),
                pltpu.VMEM((2, 7, BLK, BLK), BF16),
                pltpu.VMEM((2, 7, BLK, BLK), F32),
                pltpu.VMEM((2, NB, BLK, BLK), BF16),
                pltpu.VMEM((2, NB, BLK, BLK), BF16),
                pltpu.VMEM((CROSS, 2) + quarter, F32),
                pltpu.VMEM((CROSS,) + quarter, F32),
                pltpu.VMEM((CROSS,) + quarter, F32),
                pltpu.VMEM((2,) + quarter, F32),
                pltpu.VMEM(quarter, F32),
                pltpu.VMEM((2,) + quarter, F32),
                pltpu.VMEM((2, 7, 32, BLK), F32),
                pltpu.VMEM((1, 3, 32, BLK), F32),
                pltpu.VMEM((3, 32, BLK), F32),
                pltpu.VMEM((4, 32, BLK), F32),
                pltpu.VMEM((2, 32, BLK), F32),
                pltpu.VMEM(quarter, F32),
                pltpu.VMEM((8, 32, BLK), F32),
                pltpu.VMEM((2,) + quarter, F32),
                pltpu.VMEM((4, LOCAL + CROSS, TOK), F32),
                pltpu.SemaphoreType.REGULAR((2,)),
                sem, sem,
                sem, sem,
                sem, sem,
                sem, sem,
                sem((2,)), sem((2,)),
                sem((1,)), sem((1,)),
                sem, sem,
                sem, sem,
                sem, sem,
                sem, sem,
                sem, sem,
                sem, sem,
            ],
            compiler_params=pltpu.CompilerParams(
                collective_id=0, has_side_effects=True, vmem_limit_bytes=40 * 2**20
            ),
        )(*[pltpu.with_memory_space_constraint(a, pltpu.HBM) for a in (queries, key_vectors, values, out_grad, level_coef, saved_states)])
    return tuple(
        pl.pallas_call(
            finish,
            out_shape=[tokens] * 3 + [coefs],
            in_specs=[vmem] * 7,
            out_specs=[hbm] * 4,
            scratch_shapes=[
                pltpu.VMEM((TOK, 2 * BLK), BF16),
                pltpu.VMEM((TOK, 2 * BLK), BF16),
                sem((2 + 2 * NB,)),
            ],
            compiler_params=pltpu.CompilerParams(vmem_limit_bytes=16 * 2**20),
        )(*parts)
    )


def solution(mesh):
    in_specs = (
        P("seq", "head"),
        P("seq", "head"),
        P("seq", "head"),
        P("seq", "head"),
        P(None, "seq"),
        P("seq", None, "head", None, None),
    )
    out_specs = (P("seq", "head"), P("seq", "head"), P("seq", "head"), P(None, "seq"))
    return jax.shard_map(shards, mesh=mesh, in_specs=in_specs, out_specs=out_specs, check_vma=False)
```
